32 devices in a mesh: groups: 2 (over x), stream: 8 (over z, y), section: 2 (over core).
Axes of the slice: x: 2, y: 2, z: 4, core: 2. Of those that a mesh axis runs over, the one named last changes fastest.
Arguments:
- new_frames: bfloat16 [256, 16, 1024], P(('groups', 'stream')), parts along dimension 0, may hold values from -6 to 6
- valid_counts: int32 [256], P('groups'), parts along dimension 0, may hold values from 1 to 16
- anchor: int32 [256], P('groups'), parts along dimension 0, may hold values from 0 to 127, as said below
- context_cache: bfloat16 [2, 256, 12, 2048], P('section', ('groups', 'stream')), parts along dimension 1, may hold values from -240 to 240
- conv_state: bfloat16 [2, 256, 30, 1024], P('section', ('groups', 'stream')), parts along dimension 1, may hold values from -6 to 6
- qkv_weight: bfloat16 [2, 1024, 3072], P('section'), may hold values from -0.1875 to 0.1875
- out_weight: bfloat16 [2, 1024, 1024], P('section'), may hold values from -0.1875 to 0.1875
- conv_weight: float32 [2, 31, 1024], P('section'), may hold values from -1 to 1
Outputs:
- layer_outputs: bfloat16 [2, 256, 16, 1024], P('section', ('groups', 'stream')), parts along dimension 1
The draws below stay inside these ranges and needn't reach their ends.
There are 2 independent parts, one for each index of `groups`. The reference program is written for one: setup_inputs(seed, part) draws one part's arguments, and reference() takes and returns one part's arrays. A program takes and returns all parts, laid end to end along the dimension named above; an argument that names none is the same for every part. Nothing has to cross between parts.
Inputs may be any that keep to these rules, and one draw needn't show every extreme that they name: anchor is a permutation of the 128 slots. New slot j lies on host j // 16, old slot o on host o // 16. Exactly 7 streams leave each host and 7 arrive at it; from one old host to one other new host moves at most one stream. A stream that stays on its host keeps its slot.
All inputs are finite; a program needn't handle non-finite values.
Results may differ from the reference program's by a relative error of at most 0.0094.
Values may be sent and summed in bfloat16 or wider, within the bound.
A program may use at most 128 MiB of HBM per device.

```python
import jax
import jax.numpy as jnp
from jax import lax

D = 1024
HEADS = 16
KW = 31
FRAMES = 16
CTX = 12
S_DEV = 16
HOSTS = 8
MOVE = 7
STREAMS = 128
LAYERS = 2


def draw_anchor(key, part):
    key_label, key_offset, key_local = jax.random.split(jax.random.fold_in(key, 3), 3)
    relabel = jax.random.permutation(key_label, HOSTS).astype(jnp.int32)
    inverse = jnp.argsort(relabel).astype(jnp.int32)
    offsets = (jax.random.permutation(key_offset, HOSTS - 1).astype(jnp.int32) + 1)[:MOVE]
    local_keys = jax.random.randint(key_local, (HOSTS, S_DEV), 0, 1024, dtype=jnp.int32) * S_DEV + jnp.arange(S_DEV, dtype=jnp.int32)[None, :]
    movers = jnp.argsort(local_keys, axis=1).astype(jnp.int32)[:, :MOVE]
    host_ids = jnp.arange(HOSTS, dtype=jnp.int32)
    source = relabel[(inverse[:, None] - offsets[None, :]) % HOSTS]
    mover_ids = jnp.arange(MOVE, dtype=jnp.int32)[None, :]
    target_slots = host_ids[:, None] * S_DEV + movers
    source_slots = source * S_DEV + movers[source, mover_ids]
    anchor = jnp.arange(STREAMS, dtype=jnp.int32)
    anchor = anchor.at[target_slots.reshape(-1)].set(source_slots.reshape(-1).astype(jnp.int32))
    return anchor.astype(jnp.int32)


def draw_context_cache(key, part):
    key_base = jax.random.fold_in(jax.random.fold_in(key, 7), 0)
    entries = jnp.clip(jax.random.normal(key_base, (LAYERS, STREAMS, CTX, 2 * D), jnp.float32), -6.0, 6.0)
    return entries.astype(jnp.bfloat16)


def touch_ends(values, own_key, low, top_value):
    dims = values.shape
    index_at = [jax.random.randint(jax.random.fold_in(own_key, axis), (), 0, dims[axis]) for axis in range(len(dims))]
    values = values.at[tuple(index_at)].set(low)
    longest = dims.index(max(dims))
    index_at[longest] = (index_at[longest] + 1) % dims[longest]
    return values.at[tuple(index_at)].set(top_value)


def steps_of(own_key, shape, cuts, smallest, top_value):
    level, own = 1.0, jax.random.fold_in(own_key, 6)
    for axis_at, blocks in cuts:
        draws = jnp.exp(jax.random.uniform(jax.random.fold_in(own, axis_at), (blocks,), jnp.float32, smallest / len(cuts), top_value / len(cuts)))
        level = level * jnp.repeat(draws, shape[axis_at] // blocks).reshape([-1 if axis == axis_at else 1 for axis in range(len(shape))])
    return level


def normal_values(key, extent, spread, reach, cuts=(), kind=jnp.bfloat16):
    level = steps_of(key, extent, cuts, -0.22, 0.18) if cuts else 1.0
    result = jax.random.normal(key, extent, jnp.float32) * spread * level
    return jnp.minimum(jnp.maximum(result, -reach), reach).astype(kind)


def setup_inputs(seed: int = 0, part: int = 0) -> dict:
    streams_of = jax.random.split(jax.random.key(seed), 9)
    part_splits = jax.random.split(jax.random.fold_in(streams_of[8], part), 9)
    new_frames = normal_values(part_splits[0], (STREAMS, FRAMES, D), 1.0, 6.0, ((0, 8),))
    valid_counts = touch_ends(jax.random.randint(part_splits[1], (STREAMS,), 1, FRAMES + 1), jax.random.fold_in(part_splits[1], 1), 1, FRAMES).astype(jnp.int32)
    anchor = draw_anchor(jax.random.fold_in(jax.random.fold_in(streams_of[8], part), 71), part)
    context_cache = draw_context_cache(jax.random.fold_in(jax.random.fold_in(streams_of[8], part), 71), part)
    conv_state = normal_values(part_splits[4], (LAYERS, STREAMS, KW - 1, D), 1.0, 6.0, ((0, 2), (1, 8)))
    qkv_weight = normal_values(streams_of[5], (LAYERS, D, 3 * D), D ** -0.5, 0.1875, ((0, 2),))
    out_weight = normal_values(streams_of[6], (LAYERS, D, D), D ** -0.5, 0.1875, ((0, 2),))
    conv_weight = normal_values(streams_of[7], (LAYERS, KW, D), KW ** -0.5, 1.0, ((0, 2),), jnp.float32)
    return dict(new_frames=new_frames, valid_counts=valid_counts, anchor=anchor, context_cache=context_cache, conv_state=conv_state, qkv_weight=qkv_weight, out_weight=out_weight, conv_weight=conv_weight)


def encoder_layer(inputs, valid_counts, context, conv_state, qkv_weight, out_weight, conv_weight):
    stream_count, frame_count, model_width = inputs.shape
    head_size = model_width // HEADS
    live_mask = jnp.arange(frame_count, dtype=jnp.int32)[None, :] < valid_counts[:, None]
    floats = inputs.astype(jnp.float32)
    centred = floats - lax.optimization_barrier(jnp.mean(floats, axis=-1, keepdims=True))
    variance = lax.optimization_barrier(jnp.mean(centred * centred, axis=-1, keepdims=True))
    normed = (centred * lax.rsqrt(variance + 1e-05)).astype(jnp.bfloat16)
    projected = jnp.dot(normed.reshape(-1, model_width), qkv_weight, preferred_element_type=jnp.float32)
    projected = projected.reshape(stream_count, frame_count, 3 * model_width)
    queries = (projected[:, :, :model_width] * head_size ** (-0.5)).astype(jnp.bfloat16)
    new_keys = projected[:, :, model_width:2 * model_width].astype(jnp.bfloat16)
    new_values = projected[:, :, 2 * model_width:].astype(jnp.bfloat16)
    keys_all = jnp.concatenate([context[:, :, :model_width], new_keys], axis=1)
    values_all = jnp.concatenate([context[:, :, model_width:], new_values], axis=1)
    key_total = keys_all.shape[1]
    queries_split = queries.reshape(stream_count, frame_count, HEADS, head_size).astype(jnp.float32)
    keys_split = keys_all.reshape(stream_count, key_total, HEADS, head_size).astype(jnp.float32)
    values_split = values_all.reshape(stream_count, key_total, HEADS, head_size).astype(jnp.float32)
    scores = jnp.einsum('bqhd,bkhd->bhqk', queries_split, keys_split)
    key_mask = jnp.concatenate([jnp.ones((stream_count, key_total - frame_count), dtype=bool), live_mask], axis=1)
    scores = jnp.where(key_mask[:, None, None, :], scores, jnp.float32(-1e+30))
    top_score = lax.optimization_barrier(jnp.max(scores, axis=-1, keepdims=True))
    exponent = jnp.exp(scores - top_score)
    softmax_weights = (exponent / lax.optimization_barrier(jnp.sum(exponent, axis=-1, keepdims=True))).astype(jnp.bfloat16)
    attended = jnp.einsum('bhqk,bkhd->bqhd', softmax_weights.astype(jnp.float32), values_split)
    attended = attended.reshape(stream_count * frame_count, model_width).astype(jnp.bfloat16)
    mixed = jnp.dot(attended, out_weight, preferred_element_type=jnp.float32)
    residual_sum = floats + mixed.reshape(stream_count, frame_count, model_width)
    rounded = lax.optimization_barrier(residual_sum.astype(jnp.bfloat16))
    padded_input = jnp.concatenate([conv_state, rounded], axis=1).astype(jnp.float32)
    convolved = jnp.zeros((stream_count, frame_count, model_width), jnp.float32)
    for tap_index in range(conv_weight.shape[0]):
        convolved = convolved + conv_weight[tap_index][None, None, :] * padded_input[:, tap_index:tap_index + frame_count, :]
    output = (residual_sum + jax.nn.silu(convolved)) * live_mask[:, :, None].astype(jnp.float32)
    return output.astype(jnp.bfloat16)

def reference(new_frames, valid_counts, anchor, context_cache, conv_state, qkv_weight, out_weight, conv_weight):
    current = new_frames
    results = []
    for layer_index in range(LAYERS):
        moved_context = jnp.take(context_cache[layer_index], anchor, axis=0)
        moved_conv = jnp.take(conv_state[layer_index], anchor, axis=0)
        current = encoder_layer(current, valid_counts, moved_context, moved_conv, qkv_weight[layer_index], out_weight[layer_index], conv_weight[layer_index])
        results.append(current)
    return jnp.stack(results)
```

```python
import functools

import jax
import jax.numpy as jnp
from jax import lax
from jax.experimental import pallas as pl
from jax.experimental.pallas import tpu as pltpu
from jax.sharding import PartitionSpec as P

HEADS = 16
CHUNK = 8
MESH = pl.DeviceIdType.MESH


def kernel(
    hosts, streams, frames, width, ctx_rows, kept_rows, taps,
    anchor, valid, x_hbm, ctx_hbm, kept_hbm, wqkv_hbm, wout_hbm, wconv_hbm, out_ref,
    x_v, ctx_v, kept_v, wqkv, wout, wconv,
    x_send, x_recv, y_send, y_recv, x_work, y_work,
    normed, q_buf, k_buf, v_buf, att_buf, bias, res_buf, pad_t, conv_t,
    t_send, t_old, rank, perm, host_of, count_of,
    load_sem, xs_sem, xr_sem, ys_sem, yr_sem, hs_sem, hr_sem,
):
    me = lax.axis_index("stream")
    section = lax.axis_index("section")
    base = me * streams
    rows = CHUNK * frames
    chunks = streams // CHUNK
    group = 4
    half = group * frames
    lanes = 128

    loads = [
        pltpu.make_async_copy(x_hbm, x_v, load_sem.at[0]),
        pltpu.make_async_copy(kept_hbm.at[0], kept_v, load_sem.at[1]),
        pltpu.make_async_copy(ctx_hbm.at[0], ctx_v, load_sem.at[2]),
        pltpu.make_async_copy(wconv_hbm.at[0], wconv, load_sem.at[3]),
        pltpu.make_async_copy(wqkv_hbm.at[0], wqkv, load_sem.at[4]),
        pltpu.make_async_copy(wout_hbm.at[0], wout, load_sem.at[5]),
    ]
    for load in loads:
        load.start()

    barrier = pltpu.get_barrier_semaphore()

    def greet(step, _):
        pl.semaphore_signal(
            barrier, inc=1, device_id={"stream": lax.rem(me + step, hosts)}, device_id_type=MESH
        )
        return 0

    lax.fori_loop(1, hosts, greet, 0)
    pl.semaphore_signal(barrier, inc=1, device_id={"section": 1 - section}, device_id_type=MESH)

    def scan_send(h, _):
        found = jnp.int32(0)
        for i in range(streams):
            found = jnp.where(anchor[base + i] // streams == h, i, found)
        t_send[h] = found
        return 0

    lax.fori_loop(0, hosts, scan_send, 0)
    loads[0].wait()
    pl.semaphore_wait(barrier, hosts)

    def x_copy(to):
        return pltpu.make_async_remote_copy(
            src_ref=x_send.at[to], dst_ref=x_recv.at[me],
            send_sem=xs_sem.at[to], recv_sem=xr_sem.at[me],
            device_id={"stream": to}, device_id_type=MESH,
        )

    def x_arrival(source):
        return pltpu.make_async_remote_copy(
            src_ref=x_send.at[source], dst_ref=x_recv.at[source],
            send_sem=xs_sem.at[source], recv_sem=xr_sem.at[source],
            device_id={"stream": source}, device_id_type=MESH,
        )

    def y_copy(to):
        return pltpu.make_async_remote_copy(
            src_ref=y_send.at[to], dst_ref=y_recv.at[me],
            send_sem=ys_sem.at[to], recv_sem=yr_sem.at[me],
            device_id={"stream": to}, device_id_type=MESH,
        )

    def y_arrival(source):
        return pltpu.make_async_remote_copy(
            src_ref=y_send.at[source], dst_ref=y_recv.at[source],
            send_sem=ys_sem.at[source], recv_sem=yr_sem.at[source],
            device_id={"stream": source}, device_id_type=MESH,
        )

    def hand_over(chunk):
        span = pl.ds(chunk * CHUNK, CHUNK)
        return pltpu.make_async_remote_copy(
            src_ref=y_work.at[span], dst_ref=x_work.at[span],
            send_sem=hs_sem.at[chunk], recv_sem=hr_sem.at[chunk],
            device_id={"section": 1 - section}, device_id_type=MESH,
        )

    @pl.when(section == 0)
    def _():
        def send(step, _):
            to = lax.rem(me + step, hosts)
            x_send[to] = x_v[t_send[to]]
            x_copy(to).start()
            return 0

        lax.fori_loop(1, hosts, send, 0)

    def scan_old(h, _):
        found = jnp.int32(-1)
        for i in range(streams):
            slot = anchor[h * streams + i]
            found = jnp.where(slot // streams == me, slot - base, found)
        t_old[h] = jnp.where(h == me, -1, found)
        return 0

    lax.fori_loop(0, hosts, scan_old, 0)
    stays = [anchor[base + i] // streams == me for i in range(streams)]
    moved = jnp.int32(0)
    for i in range(streams):
        moved = moved + jnp.where(stays[i], 0, 1)
    gone, left = jnp.int32(0), moved
    for i in range(streams):
        rank[i] = jnp.where(stays[i], left, gone)
        left = left + jnp.where(stays[i], 1, 0)
        gone = gone + jnp.where(stays[i], 0, 1)

    def scan_perm(k, _):
        old = jnp.int32(0)
        for i in range(streams):
            old = jnp.where(rank[i] == k, i, old)
        perm[k] = old

        def scan_host(h, found):
            return jnp.where(t_old[h] == old, h, found)

        source = lax.fori_loop(0, hosts, scan_host, me)
        host_of[k] = source

        def scan_count(i, found):
            slot = source * streams + i
            return jnp.where(anchor[slot] == base + old, valid[slot], found)

        count_of[k] = lax.fori_loop(0, streams, scan_count, jnp.int32(0))
        return 0

    lax.fori_loop(0, streams, scan_perm, 0)

    loads[2].wait()
    loads[1].wait()
    loads[3].wait()

    def place(k, _):
        old = perm[k]
        g = k // group
        at = pl.multiple_of(lax.rem(k, group) * frames, frames)
        cached = ctx_v[old]
        filler = jnp.zeros((frames - ctx_rows, 2 * width), cached.dtype)
        cached = jnp.concatenate([cached, filler], axis=0)
        k_buf[g, pl.ds(at, frames), :] = cached[:, :width]
        v_buf[g, pl.ds(at, frames), :] = cached[:, width:]
        chunk = k // CHUNK
        kept = kept_v[old].astype(jnp.float32)
        for w in range(width // lanes):
            pad_t[chunk, w, pl.ds(lax.rem(k, CHUNK), kept_rows, stride=CHUNK), :] = kept[
                :, w * lanes : (w + 1) * lanes
            ]
        return 0

    lax.fori_loop(0, streams, place, 0)

    def mask_group(g, _):
        row = lax.broadcasted_iota(jnp.int32, (2 * half, 2 * half), 0)
        col = lax.broadcasted_iota(jnp.int32, (2 * half, 2 * half), 1)
        col_stream = lax.rem(col // frames, group)
        limit = jnp.full((2 * half, 2 * half), ctx_rows, jnp.int32)
        for i in range(group):
            limit = jnp.where((col >= half) & (col_stream == i), count_of[g * group + i], limit)
        open_ = (lax.rem(row // frames, group) == col_stream) & (lax.rem(col, frames) < limit)
        bias[g] = jnp.where(open_, 0.0, -1e30)
        return 0

    lax.fori_loop(0, streams // group, mask_group, 0)

    def conv_kept(step, _):
        chunk = step // (width // lanes)
        w = lax.rem(step, width // lanes)
        at = pl.ds(pl.multiple_of(w * lanes, lanes), lanes)
        total = jnp.zeros((rows, lanes), jnp.float32)
        for j in range(kept_rows):
            n = min(frames, kept_rows - j) * CHUNK
            term = wconv[pl.ds(j, 1), at] * pad_t[chunk, w, pl.ds(j * CHUNK, n), :]
            if n < rows:
                total = jnp.concatenate([total[:n] + term, total[n:]], axis=0)
            else:
                total = total + term
        conv_t[chunk, w] = total
        return 0

    lax.fori_loop(0, chunks * (width // lanes), conv_kept, 0)

    def project(chunk):
        x = x_work[pl.ds(chunk * CHUNK, CHUNK)].reshape(rows, width).astype(jnp.float32)
        centred = x - jnp.mean(x, axis=-1, keepdims=True)
        variance = jnp.mean(centred * centred, axis=-1, keepdims=True)
        normed[...] = (centred * lax.rsqrt(variance + 1e-05)).astype(jnp.bfloat16)
        tile = 512

        def step_of(part):
            def step(i, _):
                at = pl.multiple_of(i * tile, tile)
                got = jnp.dot(
                    normed[...], wqkv[:, pl.ds(part * width + at, tile)],
                    preferred_element_type=jnp.float32,
                )
                if part == 0:
                    q_buf[chunk, :, pl.ds(at, tile)] = (
                        got * (width // HEADS) ** (-0.5)
                    ).astype(jnp.bfloat16)
                else:
                    got = got.astype(jnp.bfloat16)
                    to = k_buf if part == 1 else v_buf
                    for g in range(CHUNK // group):
                        to[chunk * (CHUNK // group) + g, pl.ds(half, half), pl.ds(at, tile)] = got[
                            g * half : (g + 1) * half
                        ]
                return 0

            return step

        for part in range(3):
            lax.fori_loop(0, width // tile, step_of(part), 0)

    def finish(chunk):
        def attend(g, _):
            lane = lax.broadcasted_iota(jnp.int32, (half, lanes), 1)
            first = lane < lanes // 2
            whole = chunk * (CHUNK // group) + g
            at_rows = pl.ds(pl.multiple_of(g * half, half), half)
            mask = bias[whole]

            def pair(p, _):
                at = pl.ds(pl.multiple_of(p * lanes, lanes), lanes)
                q = q_buf[chunk, at_rows, at]
                none = jnp.zeros_like(q)
                q = jnp.concatenate([jnp.where(first, q, none), jnp.where(first, none, q)], axis=0)
                scores = lax.dot_general(
                    q, k_buf[whole, :, at], (((1,), (1,)), ((), ())),
                    preferred_element_type=jnp.float32,
                ) + mask
                power = jnp.exp(scores - jnp.max(scores, axis=-1, keepdims=True))
                weights = power / jnp.sum(power, axis=-1, keepdims=True)
                mixed = jnp.dot(
                    weights.astype(jnp.bfloat16), v_buf[whole, :, at],
                    preferred_element_type=jnp.float32,
                )
                att_buf[at_rows, at] = jnp.where(first, mixed[:half], mixed[half:]).astype(
                    jnp.bfloat16
                )
                return 0

            lax.fori_loop(0, width // lanes, pair, 0, unroll=True)
            return 0

        lax.fori_loop(0, CHUNK // group, attend, 0)
        tile = 256

        def mix(i, _):
            at = pl.ds(pl.multiple_of(i * tile, tile), tile)
            got = jnp.dot(att_buf[...], wout[:, at], preferred_element_type=jnp.float32)
            x = x_work[pl.ds(chunk * CHUNK, CHUNK), :, at].reshape(rows, tile)
            res_buf[:, at] = x.astype(jnp.float32) + got
            return 0

        lax.fori_loop(0, width // tile, mix, 0)

        def spread(s, _):
            own = res_buf[pl.ds(pl.multiple_of(s * frames, frames), frames), :]
            own = own.astype(jnp.bfloat16).astype(jnp.float32)
            for w in range(width // lanes):
                pad_t[chunk, w, pl.ds(kept_rows * CHUNK + s, frames, stride=CHUNK), :] = own[
                    :, w * lanes : (w + 1) * lanes
                ]
            return 0

        lax.fori_loop(0, CHUNK, spread, 0)

        def conv_new(step, _):
            at = pl.ds(pl.multiple_of(step * lanes, lanes), lanes)
            total = conv_t[chunk, step]
            for j in range(taps - frames, taps):
                start = (kept_rows - j) * CHUNK
                n = rows - start
                term = wconv[pl.ds(j, 1), at] * pad_t[chunk, step, pl.ds(kept_rows * CHUNK, n), :]
                if start:
                    total = jnp.concatenate([total[:start], total[start:] + term], axis=0)
                else:
                    total = total + term
            conv_t[chunk, step] = total / (1.0 + jnp.exp(-total))
            return 0

        lax.fori_loop(0, width // lanes, conv_new, 0)

        def close(s, _):
            k = chunk * CHUNK + s
            own = res_buf[pl.ds(pl.multiple_of(s * frames, frames), frames), :]
            own = own + jnp.concatenate(
                [
                    conv_t[chunk, w, pl.ds(s, frames, stride=CHUNK), :]
                    for w in range(width // lanes)
                ],
                axis=1,
            )
            frame = lax.broadcasted_iota(jnp.int32, (frames, width), 0)
            y_work[k] = jnp.where(frame < count_of[k], own, 0.0).astype(jnp.bfloat16)
            return 0

        lax.fori_loop(0, CHUNK, close, 0)

    @pl.when(section == 0)
    def _():
        def stayer(k, _):
            x_work[k] = x_v[perm[k]]
            return 0

        lax.fori_loop(CHUNK, streams, stayer, 0)

    loads[4].wait()

    @pl.when(section == 0)
    def _():
        project(1)

        def arrive(step, _):
            x_arrival(lax.rem(me + step, hosts)).wait_recv()
            return 0

        lax.fori_loop(1, hosts, arrive, 0)

        def mover(k, _):
            source = host_of[k]
            x_work[k] = jnp.where(source == me, x_v[perm[k]], x_recv[source])
            return 0

        lax.fori_loop(0, CHUNK, mover, 0)

    @pl.when(section == 1)
    def _():
        hand_over(0).wait_recv()

    project(0)
    loads[5].wait()
    finish(0)

    @pl.when(section == 0)
    def _():
        hand_over(0).start()

    def give_back(step, _):
        to = lax.rem(me + step, hosts)
        y_send[to] = y_work[rank[jnp.maximum(t_old[to], 0)]]
        y_copy(to).start()
        return 0

    lax.fori_loop(1, hosts, give_back, 0)

    @pl.when(section == 1)
    def _():
        hand_over(1).wait_recv()
        project(1)

    finish(1)

    @pl.when(section == 0)
    def _():
        hand_over(1).start()

    def returned(step, _):
        y_arrival(lax.rem(me + step, hosts)).wait_recv()
        return 0

    lax.fori_loop(1, hosts, returned, 0)

    def assemble(i, _):
        source = anchor[base + i] // streams
        out_ref[0, i] = jnp.where(source == me, y_work[rank[i]], y_recv[source])
        return 0

    lax.fori_loop(0, streams, assemble, 0)

    def sent(step, _):
        y_copy(lax.rem(me + step, hosts)).wait_send()
        return 0

    lax.fori_loop(1, hosts, sent, 0)

    @pl.when(section == 0)
    def _():
        def x_sent(step, _):
            x_copy(lax.rem(me + step, hosts)).wait_send()
            return 0

        lax.fori_loop(1, hosts, x_sent, 0)
        hand_over(0).wait_send()
        hand_over(1).wait_send()


def body(new_frames, valid, anchor, context, kept, wqkv, wout, wconv):
    streams, frames, width = new_frames.shape
    hosts = lax.axis_size("stream")
    ctx_rows, kept_rows, taps = context.shape[2], kept.shape[2], wconv.shape[1]
    assert streams == 2 * CHUNK and lax.axis_size("section") == 2
    assert frames == 16 and taps == kept_rows + 1
    chunks, groups = streams // CHUNK, streams // 4
    rows = CHUNK * frames
    bf16, f32, i32 = jnp.bfloat16, jnp.float32, jnp.int32
    vmem, smem = pltpu.VMEM, pltpu.SMEM
    dma = pltpu.SemaphoreType.DMA
    call = pl.pallas_call(
        functools.partial(kernel, hosts, streams, frames, width, ctx_rows, kept_rows, taps),
        out_shape=jax.ShapeDtypeStruct((1, streams, frames, width), bf16),
        in_specs=[pl.BlockSpec(memory_space=pltpu.SMEM)] * 2
        + [pl.BlockSpec(memory_space=pl.ANY)] * 6,
        out_specs=pl.BlockSpec(memory_space=pltpu.VMEM),
        scratch_shapes=[
            vmem((streams, frames, width), bf16),
            vmem((streams, ctx_rows, 2 * width), bf16),
            vmem((streams, kept_rows, width), bf16),
            vmem((width, 3 * width), bf16),
            vmem((width, width), bf16),
            vmem((taps, width), f32),
            vmem((hosts, frames, width), bf16),
            vmem((hosts, frames, width), bf16),
            vmem((hosts, frames, width), bf16),
            vmem((hosts, frames, width), bf16),
            vmem((streams, frames, width), bf16),
            vmem((streams, frames, width), bf16),
            vmem((rows, width), bf16),
            vmem((chunks, rows, width), bf16),
            vmem((groups, 8 * frames, width), bf16),
            vmem((groups, 8 * frames, width), bf16),
            vmem((rows, width), bf16),
            vmem((groups, 8 * frames, 8 * frames), f32),
            vmem((rows, width), f32),
            vmem((chunks, width // 128, (kept_rows + frames) * CHUNK, 128), f32),
            vmem((chunks, width // 128, rows, 128), f32),
            smem((hosts,), i32),
            smem((hosts,), i32),
            smem((streams,), i32),
            smem((streams,), i32),
            smem((streams,), i32),
            smem((streams,), i32),
            dma((6,)),
            dma((hosts,)),
            dma((hosts,)),
            dma((hosts,)),
            dma((hosts,)),
            dma((chunks,)),
            dma((chunks,)),
        ],
        compiler_params=pltpu.CompilerParams(
            collective_id=0, has_side_effects=True, vmem_limit_bytes=56 * 1024 * 1024
        ),
        cost_estimate=pl.CostEstimate(
            flops=2 * streams * frames * width * width * 4,
            bytes_accessed=12 * 1024 * 1024,
            transcendentals=streams * frames * width,
        ),
    )
    return call(anchor, valid, new_frames, context, kept, wqkv, wout, wconv)


def solution(mesh):
    return jax.shard_map(
        body,
        mesh=mesh,
        in_specs=(
            P(("groups", "stream"), None, None),
            P("groups"),
            P("groups"),
            P("section", ("groups", "stream"), None, None),
            P("section", ("groups", "stream"), None, None),
            P("section", None, None),
            P("section", None, None),
            P("section", None, None),
        ),
        out_specs=P("section", ("groups", "stream"), None, None),
        check_vma=False,
    )
```

```python
import functools

import jax
import jax.numpy as jnp
from jax import lax
from jax.experimental import pallas as pl
from jax.experimental.pallas import tpu as pltpu
from jax.sharding import PartitionSpec as P

HEADS = 16
CHUNK = 8
MESH = pl.DeviceIdType.MESH


def kernel(
    hosts, streams, frames, width, ctx_rows, kept_rows, taps,
    anchor, valid, x_hbm, ctx_hbm, kept_hbm, wqkv_hbm, wout_hbm, wconv_hbm, out_ref,
    x_v, ctx_v, kept_v, wqkv, wout, wconv, pick, pick_kept,
    x_send, x_recv, y_send, y_recv, x_work, y_work,
    normed, q_buf, k_buf, v_buf, att_buf, bias, res_buf, pad_t, conv_t,
    t_send, t_old, t_count, rank, perm, host_of, count_of,
    load_sem, xs_sem, xr_sem, ys_sem, yr_sem, hs_sem, hr_sem,
):
    me = lax.axis_index("stream")
    section = lax.axis_index("section")
    base = me * streams
    rows = CHUNK * frames
    chunks = streams // CHUNK
    group = 4
    half = group * frames
    lanes = 128

    loads = [
        pltpu.make_async_copy(x_hbm, x_v, load_sem.at[0]),
        pltpu.make_async_copy(kept_hbm.at[0], kept_v, load_sem.at[1]),
        pltpu.make_async_copy(ctx_hbm.at[0], ctx_v, load_sem.at[2]),
        pltpu.make_async_copy(wconv_hbm, wconv, load_sem.at[3]),
        pltpu.make_async_copy(wqkv_hbm.at[0], wqkv, load_sem.at[4]),
        pltpu.make_async_copy(wout_hbm.at[0], wout, load_sem.at[5]),
    ]
    for load in loads:
        load.start()

    barrier = pltpu.get_barrier_semaphore()

    def greet(step, _):
        pl.semaphore_signal(
            barrier, inc=1, device_id={"stream": lax.rem(me + step, hosts)}, device_id_type=MESH
        )
        return 0

    lax.fori_loop(1, hosts, greet, 0)
    pl.semaphore_signal(barrier, inc=1, device_id={"section": 1 - section}, device_id_type=MESH)

    shift = streams.bit_length() - 1
    own = [anchor[base + i] for i in range(streams)]
    own_host = [lax.shift_right_arithmetic(a, shift) for a in own]
    short = hosts <= 8

    def scan_send(h, _):
        found = jnp.int32(0)
        for i in range(streams):
            found = jnp.where(own_host[i] == h, i, found)
        t_send[h] = found
        return 0

    lax.fori_loop(0, hosts, scan_send, 0, unroll=short)
    loads[0].wait()
    pl.semaphore_wait(barrier, hosts)

    def x_copy(to):
        return pltpu.make_async_remote_copy(
            src_ref=x_send.at[to], dst_ref=x_recv.at[me],
            send_sem=xs_sem.at[to], recv_sem=xr_sem.at[me],
            device_id={"stream": to}, device_id_type=MESH,
        )

    def x_arrival(source):
        return pltpu.make_async_remote_copy(
            src_ref=x_send.at[source], dst_ref=x_recv.at[source],
            send_sem=xs_sem.at[source], recv_sem=xr_sem.at[source],
            device_id={"stream": source}, device_id_type=MESH,
        )

    def y_copy(to):
        return pltpu.make_async_remote_copy(
            src_ref=y_send.at[to], dst_ref=y_recv.at[me],
            send_sem=ys_sem.at[to], recv_sem=yr_sem.at[me],
            device_id={"stream": to}, device_id_type=MESH,
        )

    def y_arrival(source):
        return pltpu.make_async_remote_copy(
            src_ref=y_send.at[source], dst_ref=y_recv.at[source],
            send_sem=ys_sem.at[source], recv_sem=yr_sem.at[source],
            device_id={"stream": source}, device_id_type=MESH,
        )

    def hand_over(chunk):
        span = pl.ds(chunk * CHUNK, CHUNK)
        return pltpu.make_async_remote_copy(
            src_ref=y_work.at[span], dst_ref=x_work.at[span],
            send_sem=hs_sem.at[chunk], recv_sem=hr_sem.at[chunk],
            device_id={"section": 1 - section}, device_id_type=MESH,
        )

    @pl.when(section == 0)
    def _():
        def send(step, _):
            to = lax.rem(me + step, hosts)
            x_send[to] = x_v[t_send[to]]
            x_copy(to).start()
            return 0

        lax.fori_loop(1, hosts, send, 0)

    def scan_old(h, _):
        found, count = jnp.int32(-1), jnp.int32(0)
        for i in range(streams):
            slot = anchor[h * streams + i]
            hit = (lax.shift_right_arithmetic(slot, shift) == me) & (h != me)
            found = jnp.where(hit, slot - base, found)
            count = jnp.where(hit, valid[h * streams + i], count)
        t_old[h] = found
        t_count[h] = count
        return 0

    lax.fori_loop(0, hosts, scan_old, 0, unroll=short)
    stays = [(h == me).astype(jnp.int32) for h in own_host]
    moved = streams - sum(stays)
    gone, left = jnp.int32(0), moved
    ranks = []
    for i in range(streams):
        ranks.append(jnp.where(own_host[i] == me, left, gone))
        rank[i] = ranks[i]
        left = left + stays[i]
        gone = gone + 1 - stays[i]
    for k in range(streams):
        old = jnp.int32(0)
        for i in range(streams):
            old = jnp.where(ranks[i] == k, i, old)
        perm[k] = old
        count = valid[base + old]
        if k < CHUNK:

            def scan_host(h, found):
                return jnp.where(t_old[h] == old, h, found)

            source = lax.fori_loop(0, hosts, scan_host, me, unroll=short)
            host_of[k] = source
            count = jnp.where(source == me, count, t_count[source])
        count_of[k] = count

    loads[2].wait()
    loads[1].wait()
    loads[3].wait()

    span = ctx_rows * streams
    row = lax.broadcasted_iota(jnp.int32, (frames, span), 0)
    col = lax.broadcasted_iota(jnp.int32, (frames, span), 1)
    slant = col - row * streams
    for k in range(streams):
        pick[pl.ds(k * frames, frames), :] = jnp.where(slant == perm[k], 1.0, 0.0).astype(
            jnp.bfloat16
        )

    wide = 512

    def place(i, _):
        for part, to in enumerate((k_buf, v_buf)):
            at = pl.multiple_of(i * wide, wide)
            cached = ctx_v[:, :, pl.ds(part * width + at, wide)].reshape(span, wide)
            cached = jnp.dot(pick[...], cached, preferred_element_type=jnp.float32)
            cached = cached.astype(jnp.bfloat16)
            for g in range(streams // group):
                to[g, pl.ds(0, half), pl.ds(at, wide)] = cached[g * half : (g + 1) * half]
        return 0

    lax.fori_loop(0, width // wide, place, 0)

    steps = 10
    part_rows = steps * CHUNK
    sub = lax.broadcasted_iota(jnp.int32, (CHUNK, steps * streams), 0)
    col = lax.broadcasted_iota(jnp.int32, (CHUNK, steps * streams), 1)
    blocks = []
    for chunk in range(chunks):
        wanted = jnp.zeros((CHUNK, steps * streams), jnp.int32)
        for i in range(CHUNK):
            wanted = jnp.where(sub == i, perm[chunk * CHUNK + i], wanted)
        for t in range(steps):
            blocks.append(jnp.where(col - t * streams == wanted, 1.0, 0.0))
    pick_kept[...] = jnp.concatenate(blocks, axis=0).astype(jnp.bfloat16)

    def place_kept(i, _):
        at = pl.multiple_of(i * 2 * lanes, 2 * lanes)
        for b in range(kept_rows // steps):
            kept = kept_v[pl.ds(b * steps, steps), :, pl.ds(at, 2 * lanes)]
            kept = kept.reshape(steps * streams, 2 * lanes)
            kept = jnp.dot(pick_kept[...], kept, preferred_element_type=jnp.float32)
            for chunk in range(chunks):
                for w in range(2):
                    pad_t[chunk, 2 * i + w, pl.ds(b * part_rows, part_rows), :] = kept[
                        chunk * part_rows : (chunk + 1) * part_rows, w * lanes : (w + 1) * lanes
                    ]
        return 0

    lax.fori_loop(0, width // (2 * lanes), place_kept, 0)

    row = lax.broadcasted_iota(jnp.int32, (2 * half, 2 * half), 0)
    col = lax.broadcasted_iota(jnp.int32, (2 * half, 2 * half), 1)
    col_stream = lax.shift_right_arithmetic(col, frames.bit_length() - 1) & (group - 1)
    same = lax.shift_right_arithmetic(row, frames.bit_length() - 1) & (group - 1) == col_stream
    col_frame = col & (frames - 1)
    for g in range(streams // group):
        limit = jnp.full((2 * half, 2 * half), ctx_rows, jnp.int32)
        for i in range(group):
            limit = jnp.where((col >= half) & (col_stream == i), count_of[g * group + i], limit)
        bias[g] = jnp.where(same & (col_frame < limit), 0.0, -1e30)


    def conv_kept(chunk):
        def step(w, _):
            at = pl.ds(pl.multiple_of(w * lanes, lanes), lanes)
            total = jnp.zeros((rows, lanes), jnp.float32)
            for j in range(kept_rows):
                n = min(frames, kept_rows - j) * CHUNK
                term = wconv[j, :, at] * pad_t[chunk, w, pl.ds(j * CHUNK, n), :]
                if n < rows:
                    total = jnp.concatenate([total[:n] + term, total[n:]], axis=0)
                else:
                    total = total + term
            conv_t[chunk, w] = total
            return 0

        lax.fori_loop(0, width // lanes, step, 0)

    conv_kept(0)

    def project(chunk):
        x = x_work[pl.ds(chunk * CHUNK, CHUNK)].reshape(rows, width).astype(jnp.float32)
        centred = x - jnp.mean(x, axis=-1, keepdims=True)
        variance = jnp.mean(centred * centred, axis=-1, keepdims=True)
        normed[...] = (centred * lax.rsqrt(variance + 1e-05)).astype(jnp.bfloat16)
        tile = 512

        def step_of(part):
            def step(i, _):
                at = pl.multiple_of(i * tile, tile)
                got = jnp.dot(
                    normed[...], wqkv[:, pl.ds(part * width + at, tile)],
                    preferred_element_type=jnp.float32,
                )
                if part == 0:
                    q_buf[chunk, :, pl.ds(at, tile)] = (
                        got * (width // HEADS) ** (-0.5)
                    ).astype(jnp.bfloat16)
                else:
                    got = got.astype(jnp.bfloat16)
                    to = k_buf if part == 1 else v_buf
                    for g in range(CHUNK // group):
                        to[chunk * (CHUNK // group) + g, pl.ds(half, half), pl.ds(at, tile)] = got[
                            g * half : (g + 1) * half
                        ]
                return 0

            return step

        for part in range(3):
            lax.fori_loop(0, width // tile, step_of(part), 0)

    def finish(chunk):
        def attend(g, _):
            lane = lax.broadcasted_iota(jnp.int32, (half, lanes), 1)
            first = lane < lanes // 2
            whole = chunk * (CHUNK // group) + g
            at_rows = pl.ds(pl.multiple_of(g * half, half), half)
            mask = bias[whole]

            def pair(p, _):
                at = pl.ds(pl.multiple_of(p * lanes, lanes), lanes)
                q = q_buf[chunk, at_rows, at]
                none = jnp.zeros_like(q)
                q = jnp.concatenate([jnp.where(first, q, none), jnp.where(first, none, q)], axis=0)
                scores = lax.dot_general(
                    q, k_buf[whole, :, at], (((1,), (1,)), ((), ())),
                    preferred_element_type=jnp.float32,
                ) + mask
                power = jnp.exp(scores - jnp.max(scores, axis=-1, keepdims=True))
                weights = power * (1.0 / jnp.sum(power, axis=-1, keepdims=True))
                mixed = jnp.dot(
                    weights.astype(jnp.bfloat16), v_buf[whole, :, at],
                    preferred_element_type=jnp.float32,
                )
                att_buf[at_rows, at] = jnp.where(first, mixed[:half], mixed[half:]).astype(
                    jnp.bfloat16
                )
                return 0

            lax.fori_loop(0, width // lanes, pair, 0, unroll=True)
            return 0

        lax.fori_loop(0, CHUNK // group, attend, 0)
        tile = 256

        def mix(i, _):
            at = pl.ds(pl.multiple_of(i * tile, tile), tile)
            got = jnp.dot(att_buf[...], wout[:, at], preferred_element_type=jnp.float32)
            x = x_work[pl.ds(chunk * CHUNK, CHUNK), :, at].reshape(rows, tile)
            res_buf[:, at] = x.astype(jnp.float32) + got
            return 0

        lax.fori_loop(0, width // tile, mix, 0)

        def spread(s, _):
            own = res_buf[pl.ds(pl.multiple_of(s * frames, frames), frames), :]
            own = own.astype(jnp.bfloat16).astype(jnp.float32)
            for w in range(width // lanes):
                pad_t[chunk, w, pl.ds(kept_rows * CHUNK + s, frames, stride=CHUNK), :] = own[
                    :, w * lanes : (w + 1) * lanes
                ]
            return 0

        lax.fori_loop(0, CHUNK, spread, 0)

        def conv_new(step, _):
            at = pl.ds(pl.multiple_of(step * lanes, lanes), lanes)
            total = conv_t[chunk, step]
            for j in range(taps - frames, taps):
                start = (kept_rows - j) * CHUNK
                n = rows - start
                term = wconv[j, :, at] * pad_t[chunk, step, pl.ds(kept_rows * CHUNK, n), :]
                if start:
                    total = jnp.concatenate([total[:start], total[start:] + term], axis=0)
                else:
                    total = total + term
            conv_t[chunk, step] = total / (1.0 + jnp.exp(-total))
            return 0

        lax.fori_loop(0, width // lanes, conv_new, 0)

        def close(s, _):
            k = chunk * CHUNK + s
            own = res_buf[pl.ds(pl.multiple_of(s * frames, frames), frames), :]
            own = own + jnp.concatenate(
                [
                    conv_t[chunk, w, pl.ds(s, frames, stride=CHUNK), :]
                    for w in range(width // lanes)
                ],
                axis=1,
            )
            frame = lax.broadcasted_iota(jnp.int32, (frames, width), 0)
            y_work[k] = jnp.where(frame < count_of[k], own, 0.0).astype(jnp.bfloat16)
            return 0

        lax.fori_loop(0, CHUNK, close, 0)

    loads[4].wait()

    @pl.when(section == 0)
    def _():
        def arrive(step, _):
            x_arrival(lax.rem(me + step, hosts)).wait_recv()
            return 0

        lax.fori_loop(1, hosts, arrive, 0)

        def mover(k, _):
            source = host_of[k]
            x_work[k] = jnp.where(source == me, x_v[perm[k]], x_recv[source])
            return 0

        lax.fori_loop(0, CHUNK, mover, 0)

        def stayer(k, _):
            x_work[k] = x_v[perm[k]]
            return 0

        lax.fori_loop(CHUNK, streams, stayer, 0)

    @pl.when(section == 1)
    def _():
        conv_kept(1)
        hand_over(0).wait_recv()

    project(0)
    loads[5].wait()
    finish(0)

    @pl.when(section == 0)
    def _():
        hand_over(0).start()

    def give_back(step, _):
        to = lax.rem(me + step, hosts)
        y_send[to] = y_work[rank[jnp.maximum(t_old[to], 0)]]
        y_copy(to).start()
        return 0

    lax.fori_loop(1, hosts, give_back, 0)

    @pl.when(section == 0)
    def _():
        conv_kept(1)

    @pl.when(section == 1)
    def _():
        hand_over(1).wait_recv()

    project(1)
    finish(1)

    @pl.when(section == 0)
    def _():
        hand_over(1).start()

    def returned(step, _):
        y_arrival(lax.rem(me + step, hosts)).wait_recv()
        return 0

    lax.fori_loop(1, hosts, returned, 0)

    def assemble(i, _):
        source = lax.shift_right_arithmetic(anchor[base + i], shift)
        out_ref[0, i] = jnp.where(source == me, y_work[rank[i]], y_recv[source])
        return 0

    lax.fori_loop(0, streams, assemble, 0)

    def sent(step, _):
        y_copy(lax.rem(me + step, hosts)).wait_send()
        return 0

    lax.fori_loop(1, hosts, sent, 0)

    @pl.when(section == 0)
    def _():
        def x_sent(step, _):
            x_copy(lax.rem(me + step, hosts)).wait_send()
            return 0

        lax.fori_loop(1, hosts, x_sent, 0)
        hand_over(0).wait_send()
        hand_over(1).wait_send()


def body(new_frames, valid, anchor, context, kept, wqkv, wout, wconv):
    streams, frames, width = new_frames.shape
    hosts = lax.axis_size("stream")
    ctx_rows, kept_rows, taps = context.shape[2], kept.shape[2], wconv.shape[1]
    context = jnp.transpose(context, (0, 2, 1, 3))
    kept = jnp.transpose(kept, (0, 2, 1, 3))
    wconv = jnp.transpose(wconv, (1, 0, 2))
    assert streams == 2 * CHUNK and lax.axis_size("section") == 2
    assert frames == 16 and taps == kept_rows + 1 and kept_rows % 10 == 0
    assert streams & (streams - 1) == 0
    chunks, groups = streams // CHUNK, streams // 4
    rows = CHUNK * frames
    bf16, f32, i32 = jnp.bfloat16, jnp.float32, jnp.int32
    vmem, smem = pltpu.VMEM, pltpu.SMEM
    dma = pltpu.SemaphoreType.DMA
    call = pl.pallas_call(
        functools.partial(kernel, hosts, streams, frames, width, ctx_rows, kept_rows, taps),
        out_shape=jax.ShapeDtypeStruct((1, streams, frames, width), bf16),
        in_specs=[pl.BlockSpec(memory_space=pltpu.SMEM)] * 2
        + [pl.BlockSpec(memory_space=pl.ANY)] * 6,
        out_specs=pl.BlockSpec(memory_space=pltpu.VMEM),
        scratch_shapes=[
            vmem((streams, frames, width), bf16),
            vmem((ctx_rows, streams, 2 * width), bf16),
            vmem((kept_rows, streams, width), bf16),
            vmem((width, 3 * width), bf16),
            vmem((width, width), bf16),
            vmem((taps, 1, width), f32),
            vmem((streams * frames, ctx_rows * streams), bf16),
            vmem((10 * streams, 10 * streams), bf16),
            vmem((hosts, frames, width), bf16),
            vmem((hosts, frames, width), bf16),
            vmem((hosts, frames, width), bf16),
            vmem((hosts, frames, width), bf16),
            vmem((streams, frames, width), bf16),
            vmem((streams, frames, width), bf16),
            vmem((rows, width), bf16),
            vmem((chunks, rows, width), bf16),
            vmem((groups, 8 * frames, width), bf16),
            vmem((groups, 8 * frames, width), bf16),
            vmem((rows, width), bf16),
            vmem((groups, 8 * frames, 8 * frames), f32),
            vmem((rows, width), f32),
            vmem((chunks, width // 128, (kept_rows + frames) * CHUNK, 128), f32),
            vmem((chunks, width // 128, rows, 128), f32),
            smem((hosts,), i32),
            smem((hosts,), i32),
            smem((hosts,), i32),
            smem((streams,), i32),
            smem((streams,), i32),
            smem((streams,), i32),
            smem((streams,), i32),
            dma((6,)),
            dma((hosts,)),
            dma((hosts,)),
            dma((hosts,)),
            dma((hosts,)),
            dma((chunks,)),
            dma((chunks,)),
        ],
        compiler_params=pltpu.CompilerParams(
            collective_id=0, has_side_effects=True, vmem_limit_bytes=56 * 1024 * 1024
        ),
        cost_estimate=pl.CostEstimate(
            flops=2 * streams * frames * width * width * 4,
            bytes_accessed=12 * 1024 * 1024,
            transcendentals=streams * frames * width,
        ),
    )
    return call(anchor, valid, new_frames, context, kept, wqkv, wout, wconv)


def solution(mesh):
    return jax.shard_map(
        body,
        mesh=mesh,
        in_specs=(
            P(("groups", "stream"), None, None),
            P("groups"),
            P("groups"),
            P("section", ("groups", "stream"), None, None),
            P("section", ("groups", "stream"), None, None),
            P("section", None, None),
            P("section", None, None),
            P("section", None, None),
        ),
        out_specs=P("section", ("groups", "stream"), None, None),
        check_vma=False,
    )
```

```python
import functools

import jax
import jax.numpy as jnp
from jax import lax
from jax.experimental import pallas as pl
from jax.experimental.pallas import tpu as pltpu
from jax.sharding import PartitionSpec as P

HEADS = 16
CHUNK = 8
MESH = pl.DeviceIdType.MESH


def kernel(
    hosts, streams, frames, width, ctx_rows, kept_rows, taps,
    anchor, valid, x_hbm, ctx_hbm, kept_hbm, wqkv_hbm, wout_hbm, wconv_hbm, out_ref,
    x_v, ctx_v, kept_v, wqkv, wout, wconv, pick, pick_kept,
    x_send, x_recv, y_send, y_recv, x_work, y_work,
    normed, q_buf, k_buf, v_buf, att_buf, s_buf, p_buf, bias, res_buf, pad_t, conv_t,
    t_send, t_old, t_count, rank, perm, host_of, count_of,
    load_sem, xs_sem, xr_sem, ys_sem, yr_sem, hs_sem, hr_sem,
):
    me = lax.axis_index("stream")
    section = lax.axis_index("section")
    base = me * streams
    rows = CHUNK * frames
    chunks = streams // CHUNK
    group = 4
    half = group * frames
    lanes = 128

    loads = [
        pltpu.make_async_copy(x_hbm, x_v, load_sem.at[0]),
        pltpu.make_async_copy(kept_hbm.at[0], kept_v, load_sem.at[1]),
        pltpu.make_async_copy(ctx_hbm.at[0], ctx_v, load_sem.at[2]),
        pltpu.make_async_copy(wconv_hbm, wconv, load_sem.at[3]),
        pltpu.make_async_copy(wqkv_hbm.at[0], wqkv, load_sem.at[4]),
        pltpu.make_async_copy(wout_hbm.at[0], wout, load_sem.at[5]),
    ]
    for load in loads:
        load.start()

    barrier = pltpu.get_barrier_semaphore()

    def greet(step, _):
        pl.semaphore_signal(
            barrier, inc=1, device_id={"stream": lax.rem(me + step, hosts)}, device_id_type=MESH
        )
        return 0

    lax.fori_loop(1, hosts, greet, 0)
    pl.semaphore_signal(barrier, inc=1, device_id={"section": 1 - section}, device_id_type=MESH)

    shift = streams.bit_length() - 1
    own = [anchor[base + i] for i in range(streams)]
    own_host = [lax.shift_right_arithmetic(a, shift) for a in own]
    short = hosts <= 8

    def scan_send(h, _):
        found = jnp.int32(0)
        for i in range(streams):
            found = jnp.where(own_host[i] == h, i, found)
        t_send[h] = found
        return 0

    lax.fori_loop(0, hosts, scan_send, 0, unroll=short)
    loads[0].wait()
    pl.semaphore_wait(barrier, hosts)

    def x_copy(to):
        return pltpu.make_async_remote_copy(
            src_ref=x_send.at[to], dst_ref=x_recv.at[me],
            send_sem=xs_sem.at[to], recv_sem=xr_sem.at[me],
            device_id={"stream": to}, device_id_type=MESH,
        )

    def x_arrival(source):
        return pltpu.make_async_remote_copy(
            src_ref=x_send.at[source], dst_ref=x_recv.at[source],
            send_sem=xs_sem.at[source], recv_sem=xr_sem.at[source],
            device_id={"stream": source}, device_id_type=MESH,
        )

    def y_copy(to):
        return pltpu.make_async_remote_copy(
            src_ref=y_send.at[to], dst_ref=y_recv.at[me],
            send_sem=ys_sem.at[to], recv_sem=yr_sem.at[me],
            device_id={"stream": to}, device_id_type=MESH,
        )

    def y_arrival(source):
        return pltpu.make_async_remote_copy(
            src_ref=y_send.at[source], dst_ref=y_recv.at[source],
            send_sem=ys_sem.at[source], recv_sem=yr_sem.at[source],
            device_id={"stream": source}, device_id_type=MESH,
        )

    def hand_over(chunk):
        span = pl.ds(chunk * CHUNK, CHUNK)
        return pltpu.make_async_remote_copy(
            src_ref=y_work.at[span], dst_ref=x_work.at[span],
            send_sem=hs_sem.at[chunk], recv_sem=hr_sem.at[chunk],
            device_id={"section": 1 - section}, device_id_type=MESH,
        )

    @pl.when(section == 0)
    def _():
        def send(step, _):
            to = lax.rem(me + step, hosts)
            x_send[to] = x_v[t_send[to]]
            x_copy(to).start()
            return 0

        lax.fori_loop(1, hosts, send, 0)

    def scan_old(h, _):
        found, count = jnp.int32(-1), jnp.int32(0)
        for i in range(streams):
            slot = anchor[h * streams + i]
            hit = (lax.shift_right_arithmetic(slot, shift) == me) & (h != me)
            found = jnp.where(hit, slot - base, found)
            count = jnp.where(hit, valid[h * streams + i], count)
        t_old[h] = found
        t_count[h] = count
        return 0

    lax.fori_loop(0, hosts, scan_old, 0, unroll=short)
    stays = [(h == me).astype(jnp.int32) for h in own_host]
    moved = streams - sum(stays)
    gone, left = jnp.int32(0), moved
    ranks = []
    for i in range(streams):
        ranks.append(jnp.where(own_host[i] == me, left, gone))
        rank[i] = ranks[i]
        left = left + stays[i]
        gone = gone + 1 - stays[i]
    for k in range(streams):
        old = jnp.int32(0)
        for i in range(streams):
            old = jnp.where(ranks[i] == k, i, old)
        perm[k] = old
        count = valid[base + old]
        if k < CHUNK:

            def scan_host(h, found):
                return jnp.where(t_old[h] == old, h, found)

            source = lax.fori_loop(0, hosts, scan_host, me, unroll=short)
            host_of[k] = source
            count = jnp.where(source == me, count, t_count[source])
        count_of[k] = count

    loads[2].wait()
    loads[1].wait()
    loads[3].wait()

    span = ctx_rows * streams
    row = lax.broadcasted_iota(jnp.int32, (frames, span), 0)
    col = lax.broadcasted_iota(jnp.int32, (frames, span), 1)
    slant = col - row * streams
    for k in range(streams):
        pick[pl.ds(k * frames, frames), :] = jnp.where(slant == perm[k], 1.0, 0.0).astype(
            jnp.bfloat16
        )

    wide = 512

    def place(i, _):
        for part, to in enumerate((k_buf, v_buf)):
            at = pl.multiple_of(i * wide, wide)
            cached = ctx_v[:, :, pl.ds(part * width + at, wide)].reshape(span, wide)
            cached = jnp.dot(pick[...], cached, preferred_element_type=jnp.float32)
            cached = cached.astype(jnp.bfloat16)
            for g in range(streams // group):
                to[g, pl.ds(0, half), pl.ds(at, wide)] = cached[g * half : (g + 1) * half]
        return 0

    lax.fori_loop(0, width // wide, place, 0)

    steps = 10
    part_rows = steps * CHUNK
    sub = lax.broadcasted_iota(jnp.int32, (CHUNK, steps * streams), 0)
    col = lax.broadcasted_iota(jnp.int32, (CHUNK, steps * streams), 1)
    blocks = []
    for chunk in range(chunks):
        wanted = jnp.zeros((CHUNK, steps * streams), jnp.int32)
        for i in range(CHUNK):
            wanted = jnp.where(sub == i, perm[chunk * CHUNK + i], wanted)
        for t in range(steps):
            blocks.append(jnp.where(col - t * streams == wanted, 1.0, 0.0))
    pick_kept[...] = jnp.concatenate(blocks, axis=0).astype(jnp.bfloat16)

    def place_kept(i, _):
        at = pl.multiple_of(i * 2 * lanes, 2 * lanes)
        for b in range(kept_rows // steps):
            kept = kept_v[pl.ds(b * steps, steps), :, pl.ds(at, 2 * lanes)]
            kept = kept.reshape(steps * streams, 2 * lanes)
            kept = jnp.dot(pick_kept[...], kept, preferred_element_type=jnp.float32)
            for chunk in range(chunks):
                for w in range(2):
                    pad_t[chunk, 2 * i + w, pl.ds(b * part_rows, part_rows), :] = kept[
                        chunk * part_rows : (chunk + 1) * part_rows, w * lanes : (w + 1) * lanes
                    ]
        return 0

    lax.fori_loop(0, width // (2 * lanes), place_kept, 0)

    row = lax.broadcasted_iota(jnp.int32, (2 * half, 2 * half), 0)
    col = lax.broadcasted_iota(jnp.int32, (2 * half, 2 * half), 1)
    col_stream = lax.shift_right_arithmetic(col, frames.bit_length() - 1) & (group - 1)
    same = lax.shift_right_arithmetic(row, frames.bit_length() - 1) & (group - 1) == col_stream
    col_frame = col & (frames - 1)
    for g in range(streams // group):
        limit = jnp.full((2 * half, 2 * half), ctx_rows, jnp.int32)
        for i in range(group):
            limit = jnp.where((col >= half) & (col_stream == i), count_of[g * group + i], limit)
        bias[g] = jnp.where(same & (col_frame < limit), 0.0, -1e30)


    def conv_kept(chunk):
        def step(w, _):
            at = pl.ds(pl.multiple_of(w * lanes, lanes), lanes)
            total = jnp.zeros((rows, lanes), jnp.float32)
            for j in range(kept_rows):
                n = min(frames, kept_rows - j) * CHUNK
                term = wconv[j, :, at] * pad_t[chunk, w, pl.ds(j * CHUNK, n), :]
                if n < rows:
                    total = jnp.concatenate([total[:n] + term, total[n:]], axis=0)
                else:
                    total = total + term
            conv_t[chunk, w] = total
            return 0

        lax.fori_loop(0, width // lanes, step, 0)

    conv_kept(0)

    def project(chunk):
        x = x_work[pl.ds(chunk * CHUNK, CHUNK)].reshape(rows, width).astype(jnp.float32)
        centred = x - jnp.mean(x, axis=-1, keepdims=True)
        variance = jnp.mean(centred * centred, axis=-1, keepdims=True)
        normed[...] = (centred * lax.rsqrt(variance + 1e-05)).astype(jnp.bfloat16)
        tile = width

        def step_of(part):
            def step(i, _):
                at = pl.multiple_of(i * tile, tile)
                got = jnp.dot(
                    normed[...], wqkv[:, pl.ds(part * width + at, tile)],
                    preferred_element_type=jnp.float32,
                )
                if part == 0:
                    q_buf[chunk, :, pl.ds(at, tile)] = (
                        got * (width // HEADS) ** (-0.5)
                    ).astype(jnp.bfloat16)
                else:
                    got = got.astype(jnp.bfloat16)
                    to = k_buf if part == 1 else v_buf
                    for g in range(CHUNK // group):
                        to[chunk * (CHUNK // group) + g, pl.ds(half, half), pl.ds(at, tile)] = got[
                            g * half : (g + 1) * half
                        ]
                return 0

            return step

        for part in range(3):
            lax.fori_loop(0, width // tile, step_of(part), 0)

    def finish(chunk):
        def attend(g, _):
            lane = lax.broadcasted_iota(jnp.int32, (half, lanes), 1)
            first = lane < lanes // 2
            whole = chunk * (CHUNK // group) + g
            at_rows = pl.ds(pl.multiple_of(g * half, half), half)
            mask = bias[whole]

            pairs = [pl.ds(p * lanes, lanes) for p in range(width // lanes)]
            for p, at in enumerate(pairs):
                q = q_buf[chunk, at_rows, at]
                none = jnp.zeros_like(q)
                q = jnp.concatenate([jnp.where(first, q, none), jnp.where(first, none, q)], axis=0)
                s_buf[p] = lax.dot_general(
                    q, k_buf[whole, :, at], (((1,), (1,)), ((), ())),
                    preferred_element_type=jnp.float32,
                )
            for p, at in enumerate(pairs):
                scores = s_buf[p] + mask
                p_buf[p] = jnp.exp(scores - jnp.max(scores, axis=-1, keepdims=True)).astype(
                    jnp.bfloat16
                )
            ones = jnp.ones((2 * half, lanes), jnp.bfloat16)
            for p, at in enumerate(pairs):
                values = jnp.concatenate([v_buf[whole, :, at], ones], axis=1)
                mixed = jnp.dot(p_buf[p], values, preferred_element_type=jnp.float32)
                top = jnp.where(first, mixed[:half, :lanes], mixed[half:, :lanes])
                total = jnp.where(first, mixed[:half, lanes:], mixed[half:, lanes:])
                att_buf[at_rows, at] = (top / total).astype(jnp.bfloat16)
            return 0

        lax.fori_loop(0, CHUNK // group, attend, 0)
        tile = width

        def mix(i, _):
            at = pl.ds(pl.multiple_of(i * tile, tile), tile)
            got = jnp.dot(att_buf[...], wout[:, at], preferred_element_type=jnp.float32)
            x = x_work[pl.ds(chunk * CHUNK, CHUNK), :, at].reshape(rows, tile)
            res_buf[:, at] = x.astype(jnp.float32) + got
            return 0

        lax.fori_loop(0, width // tile, mix, 0)

        def spread(s, _):
            own = res_buf[pl.ds(pl.multiple_of(s * frames, frames), frames), :]
            own = own.astype(jnp.bfloat16).astype(jnp.float32)
            for w in range(width // lanes):
                pad_t[chunk, w, pl.ds(kept_rows * CHUNK + s, frames, stride=CHUNK), :] = own[
                    :, w * lanes : (w + 1) * lanes
                ]
            return 0

        lax.fori_loop(0, CHUNK, spread, 0, unroll=True)

        def conv_new(step, _):
            at = pl.ds(pl.multiple_of(step * lanes, lanes), lanes)
            total = conv_t[chunk, step]
            for j in range(taps - frames, taps):
                start = (kept_rows - j) * CHUNK
                n = rows - start
                term = wconv[j, :, at] * pad_t[chunk, step, pl.ds(kept_rows * CHUNK, n), :]
                if start:
                    total = jnp.concatenate([total[:start], total[start:] + term], axis=0)
                else:
                    total = total + term
            conv_t[chunk, step] = total / (1.0 + jnp.exp(-total))
            return 0

        lax.fori_loop(0, width // lanes, conv_new, 0)

        def close(s, _):
            k = chunk * CHUNK + s
            own = res_buf[pl.ds(pl.multiple_of(s * frames, frames), frames), :]
            own = own + jnp.concatenate(
                [
                    conv_t[chunk, w, pl.ds(s, frames, stride=CHUNK), :]
                    for w in range(width // lanes)
                ],
                axis=1,
            )
            frame = lax.broadcasted_iota(jnp.int32, (frames, width), 0)
            y_work[k] = jnp.where(frame < count_of[k], own, 0.0).astype(jnp.bfloat16)
            return 0

        lax.fori_loop(0, CHUNK, close, 0, unroll=True)

    loads[4].wait()

    @pl.when(section == 0)
    def _():
        def arrive(step, _):
            x_arrival(lax.rem(me + step, hosts)).wait_recv()
            return 0

        lax.fori_loop(1, hosts, arrive, 0)

        def mover(k, _):
            source = host_of[k]
            x_work[k] = jnp.where(source == me, x_v[perm[k]], x_recv[source])
            return 0

        lax.fori_loop(0, CHUNK, mover, 0)

        def stayer(k, _):
            x_work[k] = x_v[perm[k]]
            return 0

        lax.fori_loop(CHUNK, streams, stayer, 0)

    @pl.when(section == 1)
    def _():
        conv_kept(1)
        hand_over(0).wait_recv()

    project(0)
    loads[5].wait()
    finish(0)

    @pl.when(section == 0)
    def _():
        hand_over(0).start()

    def give_back(step, _):
        to = lax.rem(me + step, hosts)
        y_send[to] = y_work[rank[jnp.maximum(t_old[to], 0)]]
        y_copy(to).start()
        return 0

    lax.fori_loop(1, hosts, give_back, 0)

    @pl.when(section == 0)
    def _():
        conv_kept(1)

    @pl.when(section == 1)
    def _():
        hand_over(1).wait_recv()

    project(1)
    finish(1)

    @pl.when(section == 0)
    def _():
        hand_over(1).start()

    def returned(step, _):
        y_arrival(lax.rem(me + step, hosts)).wait_recv()
        return 0

    lax.fori_loop(1, hosts, returned, 0)

    def assemble(i, _):
        source = lax.shift_right_arithmetic(anchor[base + i], shift)
        out_ref[0, i] = jnp.where(source == me, y_work[rank[i]], y_recv[source])
        return 0

    lax.fori_loop(0, streams, assemble, 0)

    def sent(step, _):
        y_copy(lax.rem(me + step, hosts)).wait_send()
        return 0

    lax.fori_loop(1, hosts, sent, 0)

    @pl.when(section == 0)
    def _():
        def x_sent(step, _):
            x_copy(lax.rem(me + step, hosts)).wait_send()
            return 0

        lax.fori_loop(1, hosts, x_sent, 0)
        hand_over(0).wait_send()
        hand_over(1).wait_send()


def body(new_frames, valid, anchor, context, kept, wqkv, wout, wconv):
    streams, frames, width = new_frames.shape
    hosts = lax.axis_size("stream")
    ctx_rows, kept_rows, taps = context.shape[2], kept.shape[2], wconv.shape[1]
    context = jnp.transpose(context, (0, 2, 1, 3))
    kept = jnp.transpose(kept, (0, 2, 1, 3))
    wconv = jnp.transpose(wconv, (1, 0, 2))
    assert streams == 2 * CHUNK and lax.axis_size("section") == 2
    assert frames == 16 and taps == kept_rows + 1 and kept_rows % 10 == 0
    assert streams & (streams - 1) == 0
    chunks, groups = streams // CHUNK, streams // 4
    rows = CHUNK * frames
    bf16, f32, i32 = jnp.bfloat16, jnp.float32, jnp.int32
    vmem, smem = pltpu.VMEM, pltpu.SMEM
    dma = pltpu.SemaphoreType.DMA
    call = pl.pallas_call(
        functools.partial(kernel, hosts, streams, frames, width, ctx_rows, kept_rows, taps),
        out_shape=jax.ShapeDtypeStruct((1, streams, frames, width), bf16),
        in_specs=[pl.BlockSpec(memory_space=pltpu.SMEM)] * 2
        + [pl.BlockSpec(memory_space=pl.ANY)] * 6,
        out_specs=pl.BlockSpec(memory_space=pltpu.VMEM),
        scratch_shapes=[
            vmem((streams, frames, width), bf16),
            vmem((ctx_rows, streams, 2 * width), bf16),
            vmem((kept_rows, streams, width), bf16),
            vmem((width, 3 * width), bf16),
            vmem((width, width), bf16),
            vmem((taps, 1, width), f32),
            vmem((streams * frames, ctx_rows * streams), bf16),
            vmem((10 * streams, 10 * streams), bf16),
            vmem((hosts, frames, width), bf16),
            vmem((hosts, frames, width), bf16),
            vmem((hosts, frames, width), bf16),
            vmem((hosts, frames, width), bf16),
            vmem((streams, frames, width), bf16),
            vmem((streams, frames, width), bf16),
            vmem((rows, width), bf16),
            vmem((chunks, rows, width), bf16),
            vmem((groups, 8 * frames, width), bf16),
            vmem((groups, 8 * frames, width), bf16),
            vmem((rows, width), bf16),
            vmem((width // 128, 8 * frames, 8 * frames), f32),
            vmem((width // 128, 8 * frames, 8 * frames), bf16),
            vmem((groups, 8 * frames, 8 * frames), f32),
            vmem((rows, width), f32),
            vmem((chunks, width // 128, (kept_rows + frames) * CHUNK, 128), f32),
            vmem((chunks, width // 128, rows, 128), f32),
            smem((hosts,), i32),
            smem((hosts,), i32),
            smem((hosts,), i32),
            smem((streams,), i32),
            smem((streams,), i32),
            smem((streams,), i32),
            smem((streams,), i32),
            dma((6,)),
            dma((hosts,)),
            dma((hosts,)),
            dma((hosts,)),
            dma((hosts,)),
            dma((chunks,)),
            dma((chunks,)),
        ],
        compiler_params=pltpu.CompilerParams(
            collective_id=0, has_side_effects=True, vmem_limit_bytes=56 * 1024 * 1024
        ),
        cost_estimate=pl.CostEstimate(
            flops=2 * streams * frames * width * width * 4,
            bytes_accessed=12 * 1024 * 1024,
            transcendentals=streams * frames * width,
        ),
    )
    return call(anchor, valid, new_frames, context, kept, wqkv, wout, wconv)


def solution(mesh):
    return jax.shard_map(
        body,
        mesh=mesh,
        in_specs=(
            P(("groups", "stream"), None, None),
            P("groups"),
            P("groups"),
            P("section", ("groups", "stream"), None, None),
            P("section", ("groups", "stream"), None, None),
            P("section", None, None),
            P("section", None, None),
            P("section", None, None),
        ),
        out_specs=P("section", ("groups", "stream"), None, None),
        check_vma=False,
    )
```

```python
import functools

import jax
import jax.numpy as jnp
from jax import lax
from jax.experimental import pallas as pl
from jax.experimental.pallas import tpu as pltpu
from jax.sharding import PartitionSpec as P

HEADS = 16
CHUNK = 8
MESH = pl.DeviceIdType.MESH


def kernel(
    hosts, streams, frames, width, ctx_rows, kept_rows, taps,
    anchor, valid, x_hbm, ctx_hbm, kept_hbm, wqkv_hbm, wout_hbm, wconv_hbm, out_ref,
    x_v, ctx_v, kept_v, wqkv, wout, wconv, pick, pick_kept,
    x_send, x_recv, y_send, y_recv, x_work, y_work,
    normed, q_buf, k_buf, v_buf, att_buf, s_buf, p_buf, bias, res_buf, pad_t, conv_t,
    t_send, t_old, t_count, rank, perm, host_of, count_of,
    load_sem, xs_sem, xr_sem, ys_sem, yr_sem, hs_sem, hr_sem,
):
    me = lax.axis_index("stream")
    section = lax.axis_index("section")
    base = me * streams
    rows = CHUNK * frames
    chunks = streams // CHUNK
    group = 4
    half = group * frames
    lanes = 128

    loads = [
        pltpu.make_async_copy(x_hbm, x_v, load_sem.at[0]),
        pltpu.make_async_copy(kept_hbm.at[0], kept_v, load_sem.at[1]),
        pltpu.make_async_copy(ctx_hbm.at[0], ctx_v, load_sem.at[2]),
        pltpu.make_async_copy(wconv_hbm, wconv, load_sem.at[3]),
        pltpu.make_async_copy(wqkv_hbm.at[0], wqkv, load_sem.at[4]),
        pltpu.make_async_copy(wout_hbm.at[0], wout, load_sem.at[5]),
    ]
    loads[0].start()

    barrier = pltpu.get_barrier_semaphore()

    def greet(step, _):
        pl.semaphore_signal(
            barrier, inc=1, device_id={"stream": lax.rem(me + step, hosts)}, device_id_type=MESH
        )
        return 0

    lax.fori_loop(1, hosts, greet, 0)
    pl.semaphore_signal(barrier, inc=1, device_id={"section": 1 - section}, device_id_type=MESH)

    shift = streams.bit_length() - 1
    own = [anchor[base + i] for i in range(streams)]
    own_host = [lax.shift_right_arithmetic(a, shift) for a in own]
    short = hosts <= 8

    def scan_send(h, _):
        found = jnp.int32(0)
        for i in range(streams):
            found = jnp.where(own_host[i] == h, i, found)
        t_send[h] = found
        return 0

    lax.fori_loop(0, hosts, scan_send, 0, unroll=short)
    loads[0].wait()
    for load in loads[1:]:
        load.start()
    @pl.when(section == 0)
    def _():
        def pack(step, _):
            to = lax.rem(me + step, hosts)
            x_send[to] = x_v[t_send[to]]
            return 0

        lax.fori_loop(1, hosts, pack, 0)

    def scan_old(h, _):
        found = jnp.int32(-1)
        for i in range(streams):
            host = lax.shift_right_arithmetic(anchor[h * streams + i], shift)
            found = jnp.where(host == me, i, found)
        slot = h * streams + jnp.maximum(found, 0)
        t_old[h] = jnp.where((found >= 0) & (h != me), anchor[slot] - base, -1)
        t_count[h] = valid[slot]
        return 0

    lax.fori_loop(0, hosts, scan_old, 0, unroll=short)
    stays = [(h == me).astype(jnp.int32) for h in own_host]
    moved = streams - sum(stays)
    gone, left = jnp.int32(0), moved
    ranks = []
    for i in range(streams):
        ranks.append(jnp.where(own_host[i] == me, left, gone))
        rank[i] = ranks[i]
        left = left + stays[i]
        gone = gone + 1 - stays[i]
    for k in range(streams):
        old = jnp.int32(0)
        for i in range(streams):
            old = jnp.where(ranks[i] == k, i, old)
        perm[k] = old
        count = valid[base + old]
        if k < CHUNK:

            def scan_host(h, found):
                return jnp.where(t_old[h] == old, h, found)

            source = lax.fori_loop(0, hosts, scan_host, me, unroll=short)
            host_of[k] = source
            count = jnp.where(source == me, count, t_count[source])
        count_of[k] = count

    span = ctx_rows * streams
    row = lax.broadcasted_iota(jnp.int32, (frames, span), 0)
    col = lax.broadcasted_iota(jnp.int32, (frames, span), 1)
    slant = col - row * streams
    for k in range(streams):
        pick[pl.ds(k * frames, frames), :] = jnp.where(slant == perm[k], 1.0, 0.0).astype(
            jnp.bfloat16
        )

    steps = 10
    part_rows = steps * CHUNK
    sub = lax.broadcasted_iota(jnp.int32, (CHUNK, steps * streams), 0)
    col = lax.broadcasted_iota(jnp.int32, (CHUNK, steps * streams), 1)
    blocks = []
    for chunk in range(chunks):
        wanted = jnp.zeros((CHUNK, steps * streams), jnp.int32)
        for i in range(CHUNK):
            wanted = jnp.where(sub == i, perm[chunk * CHUNK + i], wanted)
        for t in range(steps):
            blocks.append(jnp.where(col - t * streams == wanted, 1.0, 0.0))
    pick_kept[...] = jnp.concatenate(blocks, axis=0).astype(jnp.bfloat16)

    row = lax.broadcasted_iota(jnp.int32, (2 * half, 2 * half), 0)
    col = lax.broadcasted_iota(jnp.int32, (2 * half, 2 * half), 1)
    col_stream = lax.shift_right_arithmetic(col, frames.bit_length() - 1) & (group - 1)
    same = lax.shift_right_arithmetic(row, frames.bit_length() - 1) & (group - 1) == col_stream
    col_frame = col & (frames - 1)
    for g in range(streams // group):
        limit = jnp.full((2 * half, 2 * half), ctx_rows, jnp.int32)
        for i in range(group):
            limit = jnp.where((col >= half) & (col_stream == i), count_of[g * group + i], limit)
        bias[g] = jnp.where(same & (col_frame < limit), 0.0, -1e30)


    pl.semaphore_wait(barrier, hosts)

    def x_copy(to):
        return pltpu.make_async_remote_copy(
            src_ref=x_send.at[to], dst_ref=x_recv.at[me],
            send_sem=xs_sem.at[to], recv_sem=xr_sem.at[me],
            device_id={"stream": to}, device_id_type=MESH,
        )

    def x_arrival(source):
        return pltpu.make_async_remote_copy(
            src_ref=x_send.at[source], dst_ref=x_recv.at[source],
            send_sem=xs_sem.at[source], recv_sem=xr_sem.at[source],
            device_id={"stream": source}, device_id_type=MESH,
        )

    def y_copy(to):
        return pltpu.make_async_remote_copy(
            src_ref=y_send.at[to], dst_ref=y_recv.at[me],
            send_sem=ys_sem.at[to], recv_sem=yr_sem.at[me],
            device_id={"stream": to}, device_id_type=MESH,
        )

    def y_arrival(source):
        return pltpu.make_async_remote_copy(
            src_ref=y_send.at[source], dst_ref=y_recv.at[source],
            send_sem=ys_sem.at[source], recv_sem=yr_sem.at[source],
            device_id={"stream": source}, device_id_type=MESH,
        )

    def hand_over(chunk):
        span = pl.ds(chunk * CHUNK, CHUNK)
        return pltpu.make_async_remote_copy(
            src_ref=y_work.at[span], dst_ref=x_work.at[span],
            send_sem=hs_sem.at[chunk], recv_sem=hr_sem.at[chunk],
            device_id={"section": 1 - section}, device_id_type=MESH,
        )

    @pl.when(section == 0)
    def _():
        def send(step, _):
            to = lax.rem(me + step, hosts)
            x_copy(to).start()
            return 0

        lax.fori_loop(1, hosts, send, 0)

    loads[2].wait()
    loads[1].wait()
    loads[3].wait()

    wide = 512

    def place(i, _):
        for part, to in enumerate((k_buf, v_buf)):
            at = pl.multiple_of(i * wide, wide)
            cached = ctx_v[:, :, pl.ds(part * width + at, wide)].reshape(span, wide)
            cached = jnp.dot(pick[...], cached, preferred_element_type=jnp.float32)
            cached = cached.astype(jnp.bfloat16)
            for g in range(streams // group):
                to[g, pl.ds(0, half), pl.ds(at, wide)] = cached[g * half : (g + 1) * half]
        return 0

    lax.fori_loop(0, width // wide, place, 0)

    def place_kept(i, _):
        at = pl.multiple_of(i * 2 * lanes, 2 * lanes)
        for b in range(kept_rows // steps):
            kept = kept_v[pl.ds(b * steps, steps), :, pl.ds(at, 2 * lanes)]
            kept = kept.reshape(steps * streams, 2 * lanes)
            kept = jnp.dot(pick_kept[...], kept, preferred_element_type=jnp.float32)
            for chunk in range(chunks):
                for w in range(2):
                    pad_t[chunk, 2 * i + w, pl.ds(b * part_rows, part_rows), :] = kept[
                        chunk * part_rows : (chunk + 1) * part_rows, w * lanes : (w + 1) * lanes
                    ]
        return 0

    lax.fori_loop(0, width // (2 * lanes), place_kept, 0)

    def conv_kept(chunk):
        def step(w, _):
            at = pl.ds(pl.multiple_of(w * lanes, lanes), lanes)
            total = jnp.zeros((rows, lanes), jnp.float32)
            for j in range(kept_rows):
                n = min(frames, kept_rows - j) * CHUNK
                term = wconv[j, :, at] * pad_t[chunk, w, pl.ds(j * CHUNK, n), :]
                if n < rows:
                    total = jnp.concatenate([total[:n] + term, total[n:]], axis=0)
                else:
                    total = total + term
            conv_t[chunk, w] = total
            return 0

        lax.fori_loop(0, width // lanes, step, 0)

    conv_kept(0)

    def project(chunk):
        x = x_work[pl.ds(chunk * CHUNK, CHUNK)].reshape(rows, width).astype(jnp.float32)
        centred = x - jnp.mean(x, axis=-1, keepdims=True)
        variance = jnp.mean(centred * centred, axis=-1, keepdims=True)
        normed[...] = (centred * lax.rsqrt(variance + 1e-05)).astype(jnp.bfloat16)
        tile = width

        def step_of(part):
            def step(i, _):
                at = pl.multiple_of(i * tile, tile)
                got = jnp.dot(
                    normed[...], wqkv[:, pl.ds(part * width + at, tile)],
                    preferred_element_type=jnp.float32,
                )
                if part == 0:
                    q_buf[chunk, :, pl.ds(at, tile)] = (
                        got * (width // HEADS) ** (-0.5)
                    ).astype(jnp.bfloat16)
                else:
                    got = got.astype(jnp.bfloat16)
                    to = k_buf if part == 1 else v_buf
                    for g in range(CHUNK // group):
                        to[chunk * (CHUNK // group) + g, pl.ds(half, half), pl.ds(at, tile)] = got[
                            g * half : (g + 1) * half
                        ]
                return 0

            return step

        for part in range(3):
            lax.fori_loop(0, width // tile, step_of(part), 0)

    def finish(chunk):
        def attend(g, _):
            lane = lax.broadcasted_iota(jnp.int32, (half, lanes), 1)
            first = lane < lanes // 2
            whole = chunk * (CHUNK // group) + g
            at_rows = pl.ds(pl.multiple_of(g * half, half), half)
            mask = bias[whole]

            pairs = [pl.ds(p * lanes, lanes) for p in range(width // lanes)]
            for p, at in enumerate(pairs):
                q = q_buf[chunk, at_rows, at]
                none = jnp.zeros_like(q)
                q = jnp.concatenate([jnp.where(first, q, none), jnp.where(first, none, q)], axis=0)
                s_buf[p] = lax.dot_general(
                    q, k_buf[whole, :, at], (((1,), (1,)), ((), ())),
                    preferred_element_type=jnp.float32,
                )
            for p, at in enumerate(pairs):
                scores = s_buf[p] + mask
                p_buf[p] = jnp.exp(scores - jnp.max(scores, axis=-1, keepdims=True)).astype(
                    jnp.bfloat16
                )
            ones = jnp.ones((2 * half, lanes), jnp.bfloat16)
            for p, at in enumerate(pairs):
                values = jnp.concatenate([v_buf[whole, :, at], ones], axis=1)
                mixed = jnp.dot(p_buf[p], values, preferred_element_type=jnp.float32)
                top = jnp.where(first, mixed[:half, :lanes], mixed[half:, :lanes])
                total = jnp.where(first, mixed[:half, lanes:], mixed[half:, lanes:])
                att_buf[at_rows, at] = (top / total).astype(jnp.bfloat16)
            return 0

        lax.fori_loop(0, CHUNK // group, attend, 0)
        tile = width

        def mix(i, _):
            at = pl.ds(pl.multiple_of(i * tile, tile), tile)
            got = jnp.dot(att_buf[...], wout[:, at], preferred_element_type=jnp.float32)
            x = x_work[pl.ds(chunk * CHUNK, CHUNK), :, at].reshape(rows, tile)
            res_buf[:, at] = x.astype(jnp.float32) + got
            return 0

        lax.fori_loop(0, width // tile, mix, 0)

        def spread(s, _):
            own = res_buf[pl.ds(pl.multiple_of(s * frames, frames), frames), :]
            own = own.astype(jnp.bfloat16).astype(jnp.float32)
            for w in range(width // lanes):
                pad_t[chunk, w, pl.ds(kept_rows * CHUNK + s, frames, stride=CHUNK), :] = own[
                    :, w * lanes : (w + 1) * lanes
                ]
            return 0

        lax.fori_loop(0, CHUNK, spread, 0, unroll=True)

        def conv_new(step, _):
            at = pl.ds(pl.multiple_of(step * lanes, lanes), lanes)
            total = conv_t[chunk, step]
            for j in range(taps - frames, taps):
                start = (kept_rows - j) * CHUNK
                n = rows - start
                term = wconv[j, :, at] * pad_t[chunk, step, pl.ds(kept_rows * CHUNK, n), :]
                if start:
                    total = jnp.concatenate([total[:start], total[start:] + term], axis=0)
                else:
                    total = total + term
            conv_t[chunk, step] = total / (1.0 + jnp.exp(-total))
            return 0

        lax.fori_loop(0, width // lanes, conv_new, 0)

        def close(s, _):
            k = chunk * CHUNK + s
            own = res_buf[pl.ds(pl.multiple_of(s * frames, frames), frames), :]
            own = own + jnp.concatenate(
                [
                    conv_t[chunk, w, pl.ds(s, frames, stride=CHUNK), :]
                    for w in range(width // lanes)
                ],
                axis=1,
            )
            frame = lax.broadcasted_iota(jnp.int32, (frames, width), 0)
            y_work[k] = jnp.where(frame < count_of[k], own, 0.0).astype(jnp.bfloat16)
            return 0

        lax.fori_loop(0, CHUNK, close, 0, unroll=True)

    loads[4].wait()

    @pl.when(section == 0)
    def _():
        def arrive(step, _):
            x_arrival(lax.rem(me + step, hosts)).wait_recv()
            return 0

        lax.fori_loop(1, hosts, arrive, 0)

        def mover(k, _):
            source = host_of[k]
            x_work[k] = jnp.where(source == me, x_v[perm[k]], x_recv[source])
            return 0

        lax.fori_loop(0, CHUNK, mover, 0)

        def stayer(k, _):
            x_work[k] = x_v[perm[k]]
            return 0

        lax.fori_loop(CHUNK, streams, stayer, 0)

    @pl.when(section == 1)
    def _():
        conv_kept(1)
        hand_over(0).wait_recv()

    project(0)
    loads[5].wait()
    finish(0)

    @pl.when(section == 0)
    def _():
        hand_over(0).start()

    def give_back(step, _):
        to = lax.rem(me + step, hosts)
        y_send[to] = y_work[rank[jnp.maximum(t_old[to], 0)]]
        y_copy(to).start()
        return 0

    lax.fori_loop(1, hosts, give_back, 0)

    @pl.when(section == 0)
    def _():
        conv_kept(1)

    @pl.when(section == 1)
    def _():
        hand_over(1).wait_recv()

    project(1)
    finish(1)

    @pl.when(section == 0)
    def _():
        hand_over(1).start()

    def returned(step, _):
        y_arrival(lax.rem(me + step, hosts)).wait_recv()
        return 0

    lax.fori_loop(1, hosts, returned, 0)

    def assemble(i, _):
        source = lax.shift_right_arithmetic(anchor[base + i], shift)
        out_ref[i] = jnp.where(source == me, y_work[rank[i]], y_recv[source])
        return 0

    lax.fori_loop(0, streams, assemble, 0)

    def sent(step, _):
        y_copy(lax.rem(me + step, hosts)).wait_send()
        return 0

    lax.fori_loop(1, hosts, sent, 0)

    @pl.when(section == 0)
    def _():
        def x_sent(step, _):
            x_copy(lax.rem(me + step, hosts)).wait_send()
            return 0

        lax.fori_loop(1, hosts, x_sent, 0)
        hand_over(0).wait_send()
        hand_over(1).wait_send()


def write_out(held, out_hbm, sem):
    quarter = held.shape[0] // 4
    copies = []
    for i in range(4):
        span = pl.ds(i * quarter, quarter)
        copies.append(pltpu.make_async_copy(held.at[span], out_hbm.at[0, span], sem.at[i]))
    for copy in copies:
        copy.start()
    for copy in copies:
        copy.wait()


def body(new_frames, valid, anchor, context, kept, wqkv, wout, wconv):
    streams, frames, width = new_frames.shape
    hosts = lax.axis_size("stream")
    ctx_rows, kept_rows, taps = context.shape[2], kept.shape[2], wconv.shape[1]
    context = jnp.transpose(context, (0, 2, 1, 3))
    kept = jnp.transpose(kept, (0, 2, 1, 3))
    wconv = jnp.transpose(wconv, (1, 0, 2))
    assert streams == 2 * CHUNK and lax.axis_size("section") == 2
    assert frames == 16 and taps == kept_rows + 1 and kept_rows % 10 == 0
    assert streams & (streams - 1) == 0
    chunks, groups = streams // CHUNK, streams // 4
    rows = CHUNK * frames
    bf16, f32, i32 = jnp.bfloat16, jnp.float32, jnp.int32
    vmem, smem = pltpu.VMEM, pltpu.SMEM
    dma = pltpu.SemaphoreType.DMA
    call = pl.pallas_call(
        functools.partial(kernel, hosts, streams, frames, width, ctx_rows, kept_rows, taps),
        out_shape=vmem((streams, frames, width), bf16),
        in_specs=[pl.BlockSpec(memory_space=pltpu.SMEM)] * 2
        + [pl.BlockSpec(memory_space=pl.ANY)] * 6,
        out_specs=pl.BlockSpec(memory_space=pltpu.VMEM),
        scratch_shapes=[
            vmem((streams, frames, width), bf16),
            vmem((ctx_rows, streams, 2 * width), bf16),
            vmem((kept_rows, streams, width), bf16),
            vmem((width, 3 * width), bf16),
            vmem((width, width), bf16),
            vmem((taps, 1, width), f32),
            vmem((streams * frames, ctx_rows * streams), bf16),
            vmem((10 * streams, 10 * streams), bf16),
            vmem((hosts, frames, width), bf16),
            vmem((hosts, frames, width), bf16),
            vmem((hosts, frames, width), bf16),
            vmem((hosts, frames, width), bf16),
            vmem((streams, frames, width), bf16),
            vmem((streams, frames, width), bf16),
            vmem((rows, width), bf16),
            vmem((chunks, rows, width), bf16),
            vmem((groups, 8 * frames, width), bf16),
            vmem((groups, 8 * frames, width), bf16),
            vmem((rows, width), bf16),
            vmem((width // 128, 8 * frames, 8 * frames), f32),
            vmem((width // 128, 8 * frames, 8 * frames), bf16),
            vmem((groups, 8 * frames, 8 * frames), f32),
            vmem((rows, width), f32),
            vmem((chunks, width // 128, (kept_rows + frames) * CHUNK, 128), f32),
            vmem((chunks, width // 128, rows, 128), f32),
            smem((hosts,), i32),
            smem((hosts,), i32),
            smem((hosts,), i32),
            smem((streams,), i32),
            smem((streams,), i32),
            smem((streams,), i32),
            smem((streams,), i32),
            dma((6,)),
            dma((hosts,)),
            dma((hosts,)),
            dma((hosts,)),
            dma((hosts,)),
            dma((chunks,)),
            dma((chunks,)),
        ],
        compiler_params=pltpu.CompilerParams(
            collective_id=0, has_side_effects=True, vmem_limit_bytes=56 * 1024 * 1024
        ),
        cost_estimate=pl.CostEstimate(
            flops=2 * streams * frames * width * width * 4,
            bytes_accessed=12 * 1024 * 1024,
            transcendentals=streams * frames * width,
        ),
    )
    held = call(anchor, valid, new_frames, context, kept, wqkv, wout, wconv)
    return pl.pallas_call(
        write_out,
        out_shape=jax.ShapeDtypeStruct((1, streams, frames, width), bf16),
        in_specs=[pl.BlockSpec(memory_space=pltpu.VMEM)],
        out_specs=pl.BlockSpec(memory_space=pl.ANY),
        scratch_shapes=[dma((4,))],
    )(held)


def solution(mesh):
    return jax.shard_map(
        body,
        mesh=mesh,
        in_specs=(
            P(("groups", "stream"), None, None),
            P("groups"),
            P("groups"),
            P("section", ("groups", "stream"), None, None),
            P("section", ("groups", "stream"), None, None),
            P("section", None, None),
            P("section", None, None),
            P("section", None, None),
        ),
        out_specs=P("section", ("groups", "stream"), None, None),
        check_vma=False,
    )
```

```python
import functools

import jax
import jax.numpy as jnp
from jax import lax
from jax.experimental import pallas as pl
from jax.experimental.pallas import tpu as pltpu
from jax.sharding import PartitionSpec as P

HEADS = 16
CHUNK = 4
BLOCK = 8
MESH = pl.DeviceIdType.MESH


def kernel(
    hosts, streams, frames, width, ctx_rows, kept_rows, taps,
    anchor, valid, x_hbm, ctx_hbm, kept_hbm, wqkv_hbm, wout_hbm, wconv_hbm, out_ref,
    x_v, ctx_v, kept_v, wqkv, wout, wconv, pick, pick_kept,
    x_send, x_recv, y_send, y_recv, x_work, y_work,
    normed, q_buf, k_buf, v_buf, att_buf, s_buf, p_buf, bias, res_buf, pad_t, conv_t, new_t, conv_o,
    t_send, t_old, t_count, rank, perm, host_of, count_of,
    load_sem, xs_sem, xr_sem, ys_sem, yr_sem, hs_sem, hr_sem,
):
    me = lax.axis_index("stream")
    section = lax.axis_index("section")
    base = me * streams
    rows = CHUNK * frames
    chunks = streams // CHUNK
    blocks = streams // BLOCK
    half = CHUNK * frames
    block_rows = BLOCK * frames
    lanes = 128

    loads = [
        pltpu.make_async_copy(x_hbm, x_v, load_sem.at[0]),
        pltpu.make_async_copy(kept_hbm.at[0], kept_v, load_sem.at[1]),
        pltpu.make_async_copy(ctx_hbm.at[0], ctx_v, load_sem.at[2]),
        pltpu.make_async_copy(wconv_hbm, wconv, load_sem.at[3]),
        pltpu.make_async_copy(wqkv_hbm.at[0], wqkv, load_sem.at[4]),
        pltpu.make_async_copy(wout_hbm.at[0], wout, load_sem.at[5]),
    ]
    loads[0].start()

    barrier = pltpu.get_barrier_semaphore()

    def greet(step, _):
        pl.semaphore_signal(
            barrier, inc=1, device_id={"stream": lax.rem(me + step, hosts)}, device_id_type=MESH
        )
        return 0

    lax.fori_loop(1, hosts, greet, 0)
    pl.semaphore_signal(barrier, inc=1, device_id={"section": 1 - section}, device_id_type=MESH)

    shift = streams.bit_length() - 1
    own = [anchor[base + i] for i in range(streams)]
    own_host = [lax.shift_right_arithmetic(a, shift) for a in own]
    short = hosts <= 8

    def scan_send(h, _):
        found = jnp.int32(0)
        for i in range(streams):
            found = jnp.where(own_host[i] == h, i, found)
        t_send[h] = found
        return 0

    lax.fori_loop(0, hosts, scan_send, 0, unroll=short)
    loads[0].wait()
    for load in loads[1:]:
        load.start()
    @pl.when(section == 0)
    def _():
        def pack(step, _):
            to = lax.rem(me + step, hosts)
            x_send[to] = x_v[t_send[to]]
            return 0

        lax.fori_loop(1, hosts, pack, 0)

    def scan_old(h, _):
        found = jnp.int32(-1)
        for i in range(streams):
            host = lax.shift_right_arithmetic(anchor[h * streams + i], shift)
            found = jnp.where(host == me, i, found)
        slot = h * streams + jnp.maximum(found, 0)
        t_old[h] = jnp.where((found >= 0) & (h != me), anchor[slot] - base, -1)
        t_count[h] = valid[slot]
        return 0

    lax.fori_loop(0, hosts, scan_old, 0, unroll=short)
    stays = [(h == me).astype(jnp.int32) for h in own_host]
    moved = streams - sum(stays)
    gone, left = jnp.int32(CHUNK), jnp.int32(0)
    ranks = []
    for i in range(streams):
        place_left = jnp.where(left < CHUNK, left, left + moved)
        ranks.append(jnp.minimum(jnp.where(own_host[i] == me, place_left, gone), streams - 1))
        rank[i] = ranks[i]
        left = left + stays[i]
        gone = gone + 1 - stays[i]
    for k in range(streams):
        old = jnp.int32(0)
        for i in range(streams):
            old = jnp.where(ranks[i] == k, i, old)
        perm[k] = old
        count = valid[base + old]
        if CHUNK <= k < CHUNK + BLOCK:

            def scan_host(h, found):
                return jnp.where(t_old[h] == old, h, found)

            source = lax.fori_loop(0, hosts, scan_host, me, unroll=short)
            host_of[k] = source
            count = jnp.where(source == me, count, t_count[source])
        count_of[k] = count

    span = ctx_rows * streams
    row = lax.broadcasted_iota(jnp.int32, (frames, span), 0)
    col = lax.broadcasted_iota(jnp.int32, (frames, span), 1)
    slant = col - row * streams
    for k in range(streams):
        pick[pl.ds(k * frames, frames), :] = jnp.where(slant == perm[k], 1.0, 0.0).astype(
            jnp.bfloat16
        )

    steps = 10
    part_rows = steps * BLOCK
    sub = lax.broadcasted_iota(jnp.int32, (BLOCK, steps * streams), 0)
    col = lax.broadcasted_iota(jnp.int32, (BLOCK, steps * streams), 1)
    picks = []
    for block in range(blocks):
        wanted = jnp.zeros((BLOCK, steps * streams), jnp.int32)
        for i in range(BLOCK):
            wanted = jnp.where(sub == i, perm[block * BLOCK + i], wanted)
        for t in range(steps):
            picks.append(jnp.where(col - t * streams == wanted, 1.0, 0.0))
    pick_kept[...] = jnp.concatenate(picks, axis=0).astype(jnp.bfloat16)

    row = lax.broadcasted_iota(jnp.int32, (2 * half, 2 * half), 0)
    col = lax.broadcasted_iota(jnp.int32, (2 * half, 2 * half), 1)
    col_stream = lax.shift_right_arithmetic(col, frames.bit_length() - 1) & (CHUNK - 1)
    same = lax.shift_right_arithmetic(row, frames.bit_length() - 1) & (CHUNK - 1) == col_stream
    col_frame = col & (frames - 1)
    for g in range(chunks):
        limit = jnp.full((2 * half, 2 * half), ctx_rows, jnp.int32)
        for i in range(CHUNK):
            limit = jnp.where((col >= half) & (col_stream == i), count_of[g * CHUNK + i], limit)
        bias[g] = jnp.where(same & (col_frame < limit), 0.0, -1e30)


    pl.semaphore_wait(barrier, hosts)

    def x_copy(to):
        return pltpu.make_async_remote_copy(
            src_ref=x_send.at[to], dst_ref=x_recv.at[me],
            send_sem=xs_sem.at[to], recv_sem=xr_sem.at[me],
            device_id={"stream": to}, device_id_type=MESH,
        )

    def x_arrival(source):
        return pltpu.make_async_remote_copy(
            src_ref=x_send.at[source], dst_ref=x_recv.at[source],
            send_sem=xs_sem.at[source], recv_sem=xr_sem.at[source],
            device_id={"stream": source}, device_id_type=MESH,
        )

    def y_copy(to):
        return pltpu.make_async_remote_copy(
            src_ref=y_send.at[to], dst_ref=y_recv.at[me],
            send_sem=ys_sem.at[to], recv_sem=yr_sem.at[me],
            device_id={"stream": to}, device_id_type=MESH,
        )

    def y_arrival(source):
        return pltpu.make_async_remote_copy(
            src_ref=y_send.at[source], dst_ref=y_recv.at[source],
            send_sem=ys_sem.at[source], recv_sem=yr_sem.at[source],
            device_id={"stream": source}, device_id_type=MESH,
        )

    def hand_over(chunk):
        span = pl.ds(chunk * CHUNK, CHUNK)
        return pltpu.make_async_remote_copy(
            src_ref=y_work.at[span], dst_ref=x_work.at[span],
            send_sem=hs_sem.at[chunk], recv_sem=hr_sem.at[chunk],
            device_id={"section": 1 - section}, device_id_type=MESH,
        )

    @pl.when(section == 0)
    def _():
        def send(step, _):
            to = lax.rem(me + step, hosts)
            x_copy(to).start()
            return 0

        lax.fori_loop(1, hosts, send, 0)

    loads[2].wait()
    loads[1].wait()
    loads[3].wait()

    wide = 512

    def place(i, _):
        for part, to in enumerate((k_buf, v_buf)):
            at = pl.multiple_of(i * wide, wide)
            cached = ctx_v[:, :, pl.ds(part * width + at, wide)].reshape(span, wide)
            cached = jnp.dot(pick[...], cached, preferred_element_type=jnp.float32)
            cached = cached.astype(jnp.bfloat16)
            for g in range(chunks):
                to[g, pl.ds(0, half), pl.ds(at, wide)] = cached[g * half : (g + 1) * half]
        return 0

    lax.fori_loop(0, width // wide, place, 0)

    def place_kept(i, _):
        at = pl.multiple_of(i * 2 * lanes, 2 * lanes)
        for b in range(kept_rows // steps):
            kept = kept_v[pl.ds(b * steps, steps), :, pl.ds(at, 2 * lanes)]
            kept = kept.reshape(steps * streams, 2 * lanes)
            kept = jnp.dot(pick_kept[...], kept, preferred_element_type=jnp.float32)
            for block in range(blocks):
                for w in range(2):
                    pad_t[block, 2 * i + w, pl.ds(b * part_rows, part_rows), :] = kept[
                        block * part_rows : (block + 1) * part_rows, w * lanes : (w + 1) * lanes
                    ]
        return 0

    lax.fori_loop(0, width // (2 * lanes), place_kept, 0)

    def conv_kept(block):
        def step(w, _):
            at = pl.ds(pl.multiple_of(w * lanes, lanes), lanes)
            total = jnp.zeros((block_rows, lanes), jnp.float32)
            for j in range(kept_rows):
                n = min(frames, kept_rows - j) * BLOCK
                term = wconv[j, :, at] * pad_t[block, w, pl.ds(j * BLOCK, n), :]
                if n < block_rows:
                    total = jnp.concatenate([total[:n] + term, total[n:]], axis=0)
                else:
                    total = total + term
            conv_t[block, w] = total
            return 0

        lax.fori_loop(0, width // lanes, step, 0)

    conv_kept(0)

    def project(chunk):
        x = x_work[pl.ds(chunk * CHUNK, CHUNK)].reshape(half, width).astype(jnp.float32)
        centred = x - jnp.mean(x, axis=-1, keepdims=True)
        variance = jnp.mean(centred * centred, axis=-1, keepdims=True)
        normed[...] = (centred * lax.rsqrt(variance + 1e-05)).astype(jnp.bfloat16)
        for part, to in enumerate((q_buf, k_buf, v_buf)):
            got = jnp.dot(
                normed[...], wqkv[:, part * width : (part + 1) * width],
                preferred_element_type=jnp.float32,
            )
            if part == 0:
                to[...] = (got * (width // HEADS) ** (-0.5)).astype(jnp.bfloat16)
            else:
                to[chunk, half:, :] = got.astype(jnp.bfloat16)

    def finish(chunk):
        lane = lax.broadcasted_iota(jnp.int32, (half, lanes), 1)
        first = lane < lanes // 2
        mask = bias[chunk]
        pairs = [pl.ds(p * lanes, lanes) for p in range(width // lanes)]
        for p, at in enumerate(pairs):
            q = q_buf[:, at]
            none = jnp.zeros_like(q)
            q = jnp.concatenate([jnp.where(first, q, none), jnp.where(first, none, q)], axis=0)
            s_buf[p] = lax.dot_general(
                q, k_buf[chunk, :, at], (((1,), (1,)), ((), ())),
                preferred_element_type=jnp.float32,
            )
        for p, at in enumerate(pairs):
            scores = s_buf[p] + mask
            p_buf[p] = jnp.exp(scores - jnp.max(scores, axis=-1, keepdims=True)).astype(
                jnp.bfloat16
            )
        ones = jnp.ones((2 * half, lanes), jnp.bfloat16)
        for p, at in enumerate(pairs):
            values = jnp.concatenate([v_buf[chunk, :, at], ones], axis=1)
            mixed = jnp.dot(p_buf[p], values, preferred_element_type=jnp.float32)
            top = jnp.where(first, mixed[:half, :lanes], mixed[half:, :lanes])
            total = jnp.where(first, mixed[:half, lanes:], mixed[half:, lanes:])
            att_buf[:, at] = (top / total).astype(jnp.bfloat16)

        got = jnp.dot(att_buf[...], wout[...], preferred_element_type=jnp.float32)
        x = x_work[pl.ds(chunk * CHUNK, CHUNK)].reshape(half, width).astype(jnp.float32)
        res_buf[...] = x + got

        block = lax.shift_right_arithmetic(chunk, 1)
        offset = (chunk & 1) * CHUNK
        for s in range(CHUNK):
            own = res_buf[s * frames : (s + 1) * frames, :]
            own = own.astype(jnp.bfloat16).astype(jnp.float32)
            for w in range(width // lanes):
                new_t[w, pl.ds(offset + s, frames, stride=BLOCK), :] = own[
                    :, w * lanes : (w + 1) * lanes
                ]

        def conv_new(w, _):
            at = pl.ds(pl.multiple_of(w * lanes, lanes), lanes)
            total = conv_t[block, w]
            for j in range(taps - frames, taps):
                start = (kept_rows - j) * BLOCK
                term = wconv[j, :, at] * new_t[w, pl.ds(0, block_rows - start), :]
                if start:
                    total = jnp.concatenate([total[:start], total[start:] + term], axis=0)
                else:
                    total = total + term
            conv_o[w] = total / (1.0 + jnp.exp(-total))
            return 0

        lax.fori_loop(0, width // lanes, conv_new, 0, unroll=2)

        frame = lax.broadcasted_iota(jnp.int32, (frames, width), 0)
        for s in range(CHUNK):
            k = chunk * CHUNK + s
            own = res_buf[s * frames : (s + 1) * frames, :]
            own = own + jnp.concatenate(
                [
                    conv_o[w, pl.ds(offset + s, frames, stride=BLOCK), :]
                    for w in range(width // lanes)
                ],
                axis=1,
            )
            y_work[k] = jnp.where(frame < count_of[k], own, 0.0).astype(jnp.bfloat16)

    def give_back(step, _):
        to = lax.rem(me + step, hosts)
        y_send[to] = y_work[rank[jnp.maximum(t_old[to], 0)]]
        y_copy(to).start()
        return 0

    @pl.when(section == 0)
    def _():
        for k in range(CHUNK):
            x_work[k] = x_v[perm[k]]

    @pl.when(section == 1)
    def _():
        conv_kept(1)

    loads[4].wait()
    loads[5].wait()

    def turn(chunk, _):
        @pl.when((section == 0) & (chunk == 1))
        def _():
            conv_kept(1)

            def arrive(step, _):
                x_arrival(lax.rem(me + step, hosts)).wait_recv()
                return 0

            lax.fori_loop(1, hosts, arrive, 0)

            def fill(k, _):
                x_work[k] = x_v[perm[k]]
                return 0

            def fill_moved(k, _):
                source = host_of[k]
                x_work[k] = jnp.where(source == me, x_v[perm[k]], x_recv[source])
                return 0

            lax.fori_loop(CHUNK, CHUNK + BLOCK, fill_moved, 0)
            lax.fori_loop(CHUNK + BLOCK, streams, fill, 0)

        @pl.when(section == 1)
        def _():
            hand_over(chunk).wait_recv()

        project(chunk)
        finish(chunk)

        @pl.when(section == 0)
        def _():
            hand_over(chunk).start()

        @pl.when(chunk == BLOCK // CHUNK)
        def _():
            lax.fori_loop(1, hosts, give_back, 0)

        return 0

    lax.fori_loop(0, chunks, turn, 0)

    def returned(step, _):
        y_arrival(lax.rem(me + step, hosts)).wait_recv()
        return 0

    lax.fori_loop(1, hosts, returned, 0)

    def assemble(i, _):
        source = lax.shift_right_arithmetic(anchor[base + i], shift)
        out_ref[i] = jnp.where(source == me, y_work[rank[i]], y_recv[source])
        return 0

    lax.fori_loop(0, streams, assemble, 0)

    def sent(step, _):
        y_copy(lax.rem(me + step, hosts)).wait_send()
        return 0

    lax.fori_loop(1, hosts, sent, 0)

    @pl.when(section == 0)
    def _():
        def x_sent(step, _):
            x_copy(lax.rem(me + step, hosts)).wait_send()
            return 0

        lax.fori_loop(1, hosts, x_sent, 0)
        for chunk in range(chunks):
            hand_over(chunk).wait_send()


def body(new_frames, valid, anchor, context, kept, wqkv, wout, wconv):
    streams, frames, width = new_frames.shape
    hosts = lax.axis_size("stream")
    ctx_rows, kept_rows, taps = context.shape[2], kept.shape[2], wconv.shape[1]
    context = jnp.transpose(context, (0, 2, 1, 3))
    kept = jnp.transpose(kept, (0, 2, 1, 3))
    wconv = jnp.transpose(wconv, (1, 0, 2))
    assert streams == 2 * BLOCK and BLOCK == 2 * CHUNK and lax.axis_size("section") == 2
    assert frames == 16 and taps == kept_rows + 1 and kept_rows % 10 == 0
    assert streams & (streams - 1) == 0
    chunks, blocks, tiles = streams // CHUNK, streams // BLOCK, width // 128
    rows = CHUNK * frames
    bf16, f32, i32 = jnp.bfloat16, jnp.float32, jnp.int32
    vmem, smem = pltpu.VMEM, pltpu.SMEM
    dma = pltpu.SemaphoreType.DMA
    call = pl.pallas_call(
        functools.partial(kernel, hosts, streams, frames, width, ctx_rows, kept_rows, taps),
        out_shape=vmem((streams, frames, width), bf16),
        in_specs=[pl.BlockSpec(memory_space=pltpu.SMEM)] * 2
        + [pl.BlockSpec(memory_space=pl.ANY)] * 6,
        out_specs=pl.BlockSpec(memory_space=pltpu.VMEM),
        scratch_shapes=[
            vmem((streams, frames, width), bf16),
            vmem((ctx_rows, streams, 2 * width), bf16),
            vmem((kept_rows, streams, width), bf16),
            vmem((width, 3 * width), bf16),
            vmem((width, width), bf16),
            vmem((taps, 1, width), f32),
            vmem((streams * frames, ctx_rows * streams), bf16),
            vmem((10 * streams, 10 * streams), bf16),
            vmem((hosts, frames, width), bf16),
            vmem((hosts, frames, width), bf16),
            vmem((hosts, frames, width), bf16),
            vmem((hosts, frames, width), bf16),
            vmem((streams, frames, width), bf16),
            vmem((streams, frames, width), bf16),
            vmem((rows, width), bf16),
            vmem((rows, width), bf16),
            vmem((chunks, 2 * rows, width), bf16),
            vmem((chunks, 2 * rows, width), bf16),
            vmem((rows, width), bf16),
            vmem((tiles, 2 * rows, 2 * rows), f32),
            vmem((tiles, 2 * rows, 2 * rows), bf16),
            vmem((chunks, 2 * rows, 2 * rows), f32),
            vmem((rows, width), f32),
            vmem((blocks, tiles, kept_rows * BLOCK, 128), f32),
            vmem((blocks, tiles, frames * BLOCK, 128), f32),
            vmem((tiles, frames * BLOCK, 128), f32),
            vmem((tiles, frames * BLOCK, 128), f32),
            smem((hosts,), i32),
            smem((hosts,), i32),
            smem((hosts,), i32),
            smem((streams,), i32),
            smem((streams,), i32),
            smem((streams,), i32),
            smem((streams,), i32),
            dma((6,)),
            dma((hosts,)),
            dma((hosts,)),
            dma((hosts,)),
            dma((hosts,)),
            dma((chunks,)),
            dma((chunks,)),
        ],
        compiler_params=pltpu.CompilerParams(
            collective_id=0, has_side_effects=True, vmem_limit_bytes=56 * 1024 * 1024
        ),
        cost_estimate=pl.CostEstimate(
            flops=2 * streams * frames * width * width * 4,
            bytes_accessed=12 * 1024 * 1024,
            transcendentals=streams * frames * width,
        ),
    )
    held = call(anchor, valid, new_frames, context, kept, wqkv, wout, wconv)
    return held[None]


def solution(mesh):
    return jax.shard_map(
        body,
        mesh=mesh,
        in_specs=(
            P(("groups", "stream"), None, None),
            P("groups"),
            P("groups"),
            P("section", ("groups", "stream"), None, None),
            P("section", ("groups", "stream"), None, None),
            P("section", None, None),
            P("section", None, None),
            P("section", None, None),
        ),
        out_specs=P("section", ("groups", "stream"), None, None),
        check_vma=False,
    )
```

```python
import functools

import jax
import jax.numpy as jnp
from jax import lax
from jax.experimental import pallas as pl
from jax.experimental.pallas import tpu as pltpu
from jax.sharding import PartitionSpec as P

HEADS = 16
CHUNK = 4
BLOCK = 8
LOADS = 25
MESH = pl.DeviceIdType.MESH


def kernel(
    hosts, streams, frames, width, ctx_rows, kept_rows, taps,
    anchor, valid, x_hbm, ctx_hbm, kept_hbm, wqkv_hbm, wout_hbm, wconv_hbm, out_ref,
    x_v, ctx_v, kept_v, wqkv, wout, wconv, pick, pick_kept,
    x_send, x_recv, y_send, y_recv, x_work, y_work,
    normed, q_buf, k_buf, v_buf, att_buf, s_buf, p_buf, bias, res_buf, pad_t, conv_t, new_t, conv_o,
    t_send, t_old, t_count, rank, perm, host_of, count_of,
    load_sem, xs_sem, xr_sem, ys_sem, yr_sem, hs_sem, hr_sem,
):
    me = lax.axis_index("stream")
    section = lax.axis_index("section")
    base = me * streams
    rows = CHUNK * frames
    chunks = streams // CHUNK
    blocks = streams // BLOCK
    half = CHUNK * frames
    block_rows = BLOCK * frames
    lanes = 128

    slots = iter(range(LOADS))

    def load(source, target):
        copy = pltpu.make_async_copy(source, target, load_sem.at[next(slots)])
        copy.start()
        return copy

    def load_blocks(source, target, count):
        size = target.shape[0] // count
        spans = [pl.ds(i * size, size) for i in range(count)]
        return [load(source.at[span], target.at[span]) for span in spans]

    def load_weight(source, target, part):
        at = pl.ds(part * width, width)
        return load_blocks(source.at[:, at], target.at[:, at], 4)

    def wait_for(copies):
        for copy in copies:
            copy.wait()

    x_loads = load_blocks(x_hbm, x_v, 2)
    kept_loads = load_blocks(kept_hbm.at[0], kept_v, 3)
    ctx_loads = load_blocks(ctx_hbm.at[0], ctx_v, 3)
    conv_loads = [load(wconv_hbm, wconv)]
    qkv_loads = []
    for part in range(3):
        qkv_loads += load_weight(wqkv_hbm.at[0], wqkv, part)
    out_loads = load_weight(wout_hbm.at[0], wout, 0)

    barrier = pltpu.get_barrier_semaphore()

    def greet(step, _):
        pl.semaphore_signal(
            barrier, inc=1, device_id={"stream": lax.rem(me + step, hosts)}, device_id_type=MESH
        )
        return 0

    lax.fori_loop(1, hosts, greet, 0)
    pl.semaphore_signal(barrier, inc=1, device_id={"section": 1 - section}, device_id_type=MESH)

    shift = streams.bit_length() - 1
    own = [anchor[base + i] for i in range(streams)]
    own_host = [lax.shift_right_arithmetic(a, shift) for a in own]
    short = hosts <= 8

    def scan_send(h, _):
        found = jnp.int32(0)
        for i in range(streams):
            found = jnp.where(own_host[i] == h, i, found)
        t_send[h] = found
        return 0

    lax.fori_loop(0, hosts, scan_send, 0, unroll=short)
    wait_for(x_loads)
    @pl.when(section == 0)
    def _():
        def pack(step, _):
            to = lax.rem(me + step, hosts)
            x_send[to] = x_v[t_send[to]]
            return 0

        lax.fori_loop(1, hosts, pack, 0)

    def scan_old(h, _):
        found = jnp.int32(-1)
        for i in range(streams):
            host = lax.shift_right_arithmetic(anchor[h * streams + i], shift)
            found = jnp.where(host == me, i, found)
        slot = h * streams + jnp.maximum(found, 0)
        t_old[h] = jnp.where((found >= 0) & (h != me), anchor[slot] - base, -1)
        t_count[h] = valid[slot]
        return 0

    lax.fori_loop(0, hosts, scan_old, 0, unroll=short)
    stays = [(h == me).astype(jnp.int32) for h in own_host]
    moved = streams - sum(stays)
    gone, left = jnp.int32(CHUNK), jnp.int32(0)
    ranks = []
    for i in range(streams):
        place_left = jnp.where(left < CHUNK, left, left + moved)
        ranks.append(jnp.minimum(jnp.where(own_host[i] == me, place_left, gone), streams - 1))
        rank[i] = ranks[i]
        left = left + stays[i]
        gone = gone + 1 - stays[i]
    for k in range(streams):
        old = jnp.int32(0)
        for i in range(streams):
            old = jnp.where(ranks[i] == k, i, old)
        perm[k] = old
        count = valid[base + old]
        if CHUNK <= k < CHUNK + BLOCK:

            def scan_host(h, found):
                return jnp.where(t_old[h] == old, h, found)

            source = lax.fori_loop(0, hosts, scan_host, me, unroll=short)
            host_of[k] = source
            count = jnp.where(source == me, count, t_count[source])
        count_of[k] = count

    span = ctx_rows * streams
    row = lax.broadcasted_iota(jnp.int32, (frames, span), 0)
    col = lax.broadcasted_iota(jnp.int32, (frames, span), 1)
    slant = col - row * streams
    for k in range(streams):
        pick[pl.ds(k * frames, frames), :] = jnp.where(slant == perm[k], 1.0, 0.0).astype(
            jnp.bfloat16
        )

    steps = 10
    part_rows = steps * BLOCK
    sub = lax.broadcasted_iota(jnp.int32, (BLOCK, steps * streams), 0)
    col = lax.broadcasted_iota(jnp.int32, (BLOCK, steps * streams), 1)
    picks = []
    for block in range(blocks):
        wanted = jnp.zeros((BLOCK, steps * streams), jnp.int32)
        for i in range(BLOCK):
            wanted = jnp.where(sub == i, perm[block * BLOCK + i], wanted)
        for t in range(steps):
            picks.append(jnp.where(col - t * streams == wanted, 1.0, 0.0))
    pick_kept[...] = jnp.concatenate(picks, axis=0).astype(jnp.bfloat16)

    row = lax.broadcasted_iota(jnp.int32, (2 * half, 2 * half), 0)
    col = lax.broadcasted_iota(jnp.int32, (2 * half, 2 * half), 1)
    col_stream = lax.shift_right_arithmetic(col, frames.bit_length() - 1) & (CHUNK - 1)
    same = lax.shift_right_arithmetic(row, frames.bit_length() - 1) & (CHUNK - 1) == col_stream
    col_frame = col & (frames - 1)
    for g in range(chunks):
        limit = jnp.full((2 * half, 2 * half), ctx_rows, jnp.int32)
        for i in range(CHUNK):
            limit = jnp.where((col >= half) & (col_stream == i), count_of[g * CHUNK + i], limit)
        bias[g] = jnp.where(same & (col_frame < limit), 0.0, -1e30)


    pl.semaphore_wait(barrier, hosts)

    def x_copy(to):
        return pltpu.make_async_remote_copy(
            src_ref=x_send.at[to], dst_ref=x_recv.at[me],
            send_sem=xs_sem.at[to], recv_sem=xr_sem.at[me],
            device_id={"stream": to}, device_id_type=MESH,
        )

    def x_arrival(source):
        return pltpu.make_async_remote_copy(
            src_ref=x_send.at[source], dst_ref=x_recv.at[source],
            send_sem=xs_sem.at[source], recv_sem=xr_sem.at[source],
            device_id={"stream": source}, device_id_type=MESH,
        )

    def y_copy(to):
        return pltpu.make_async_remote_copy(
            src_ref=y_send.at[to], dst_ref=y_recv.at[me],
            send_sem=ys_sem.at[to], recv_sem=yr_sem.at[me],
            device_id={"stream": to}, device_id_type=MESH,
        )

    def y_arrival(source):
        return pltpu.make_async_remote_copy(
            src_ref=y_send.at[source], dst_ref=y_recv.at[source],
            send_sem=ys_sem.at[source], recv_sem=yr_sem.at[source],
            device_id={"stream": source}, device_id_type=MESH,
        )

    def hand_over(chunk):
        span = pl.ds(chunk * CHUNK, CHUNK)
        return pltpu.make_async_remote_copy(
            src_ref=y_work.at[span], dst_ref=x_work.at[span],
            send_sem=hs_sem.at[chunk], recv_sem=hr_sem.at[chunk],
            device_id={"section": 1 - section}, device_id_type=MESH,
        )

    @pl.when(section == 0)
    def _():
        def send(step, _):
            to = lax.rem(me + step, hosts)
            x_copy(to).start()
            return 0

        lax.fori_loop(1, hosts, send, 0)

    wait_for(ctx_loads + kept_loads + conv_loads)

    wide = 512

    def place(i, _):
        for part, to in enumerate((k_buf, v_buf)):
            at = pl.multiple_of(i * wide, wide)
            cached = ctx_v[:, :, pl.ds(part * width + at, wide)].reshape(span, wide)
            cached = jnp.dot(pick[...], cached, preferred_element_type=jnp.float32)
            cached = cached.astype(jnp.bfloat16)
            for g in range(chunks):
                to[g, pl.ds(0, half), pl.ds(at, wide)] = cached[g * half : (g + 1) * half]
        return 0

    lax.fori_loop(0, width // wide, place, 0)

    def place_kept(i, _):
        at = pl.multiple_of(i * 2 * lanes, 2 * lanes)
        for b in range(kept_rows // steps):
            kept = kept_v[pl.ds(b * steps, steps), :, pl.ds(at, 2 * lanes)]
            kept = kept.reshape(steps * streams, 2 * lanes)
            kept = jnp.dot(pick_kept[...], kept, preferred_element_type=jnp.float32)
            for block in range(blocks):
                for w in range(2):
                    pad_t[block, 2 * i + w, pl.ds(b * part_rows, part_rows), :] = kept[
                        block * part_rows : (block + 1) * part_rows, w * lanes : (w + 1) * lanes
                    ]
        return 0

    lax.fori_loop(0, width // (2 * lanes), place_kept, 0)

    def conv_kept(block):
        def step(w, _):
            at = pl.ds(pl.multiple_of(w * lanes, lanes), lanes)
            total = jnp.zeros((block_rows, lanes), jnp.float32)
            for j in range(kept_rows):
                n = min(frames, kept_rows - j) * BLOCK
                term = wconv[j, :, at] * pad_t[block, w, pl.ds(j * BLOCK, n), :]
                if n < block_rows:
                    total = jnp.concatenate([total[:n] + term, total[n:]], axis=0)
                else:
                    total = total + term
            conv_t[block, w] = total
            return 0

        lax.fori_loop(0, width // lanes, step, 0)

    conv_kept(0)

    def project(chunk):
        x = x_work[pl.ds(chunk * CHUNK, CHUNK)].reshape(half, width).astype(jnp.float32)
        centred = x - jnp.mean(x, axis=-1, keepdims=True)
        variance = jnp.mean(centred * centred, axis=-1, keepdims=True)
        normed[...] = (centred * lax.rsqrt(variance + 1e-05)).astype(jnp.bfloat16)
        for part, to in enumerate((q_buf, k_buf, v_buf)):
            got = jnp.dot(
                normed[...], wqkv[:, part * width : (part + 1) * width],
                preferred_element_type=jnp.float32,
            )
            if part == 0:
                to[...] = (got * (width // HEADS) ** (-0.5)).astype(jnp.bfloat16)
            else:
                to[chunk, half:, :] = got.astype(jnp.bfloat16)

    def finish(chunk):
        lane = lax.broadcasted_iota(jnp.int32, (half, lanes), 1)
        first = lane < lanes // 2
        mask = bias[chunk]
        pairs = [pl.ds(p * lanes, lanes) for p in range(width // lanes)]
        for p, at in enumerate(pairs):
            q = q_buf[:, at]
            none = jnp.zeros_like(q)
            q = jnp.concatenate([jnp.where(first, q, none), jnp.where(first, none, q)], axis=0)
            s_buf[p] = lax.dot_general(
                q, k_buf[chunk, :, at], (((1,), (1,)), ((), ())),
                preferred_element_type=jnp.float32,
            )
        for p, at in enumerate(pairs):
            scores = s_buf[p] + mask
            p_buf[p] = jnp.exp(scores - jnp.max(scores, axis=-1, keepdims=True)).astype(
                jnp.bfloat16
            )
        ones = jnp.ones((2 * half, lanes), jnp.bfloat16)
        for p, at in enumerate(pairs):
            values = jnp.concatenate([v_buf[chunk, :, at], ones], axis=1)
            mixed = jnp.dot(p_buf[p], values, preferred_element_type=jnp.float32)
            top = jnp.where(first, mixed[:half, :lanes], mixed[half:, :lanes])
            total = jnp.where(first, mixed[:half, lanes:], mixed[half:, lanes:])
            att_buf[:, at] = (top / total).astype(jnp.bfloat16)

        got = jnp.dot(att_buf[...], wout[...], preferred_element_type=jnp.float32)
        x = x_work[pl.ds(chunk * CHUNK, CHUNK)].reshape(half, width).astype(jnp.float32)
        res_buf[...] = x + got

        block = lax.shift_right_arithmetic(chunk, 1)
        offset = (chunk & 1) * CHUNK
        for s in range(CHUNK):
            own = res_buf[s * frames : (s + 1) * frames, :]
            own = own.astype(jnp.bfloat16).astype(jnp.float32)
            for w in range(width // lanes):
                new_t[w, pl.ds(offset + s, frames, stride=BLOCK), :] = own[
                    :, w * lanes : (w + 1) * lanes
                ]

        def conv_new(w, _):
            at = pl.ds(pl.multiple_of(w * lanes, lanes), lanes)
            total = conv_t[block, w]
            for j in range(taps - frames, taps):
                start = (kept_rows - j) * BLOCK
                term = wconv[j, :, at] * new_t[w, pl.ds(0, block_rows - start), :]
                if start:
                    total = jnp.concatenate([total[:start], total[start:] + term], axis=0)
                else:
                    total = total + term
            conv_o[w] = total / (1.0 + jnp.exp(-total))
            return 0

        lax.fori_loop(0, width // lanes, conv_new, 0, unroll=2)

        frame = lax.broadcasted_iota(jnp.int32, (frames, width), 0)
        for s in range(CHUNK):
            k = chunk * CHUNK + s
            own = res_buf[s * frames : (s + 1) * frames, :]
            own = own + jnp.concatenate(
                [
                    conv_o[w, pl.ds(offset + s, frames, stride=BLOCK), :]
                    for w in range(width // lanes)
                ],
                axis=1,
            )
            y_work[k] = jnp.where(frame < count_of[k], own, 0.0).astype(jnp.bfloat16)

    def give_back(step, _):
        to = lax.rem(me + step, hosts)
        y_send[to] = y_work[rank[jnp.maximum(t_old[to], 0)]]
        y_copy(to).start()
        return 0

    @pl.when(section == 0)
    def _():
        for k in range(CHUNK):
            x_work[k] = x_v[perm[k]]

    @pl.when(section == 1)
    def _():
        conv_kept(1)

    wait_for(qkv_loads)

    def turn(chunk, _):
        @pl.when((section == 0) & (chunk == 1))
        def _():
            conv_kept(1)

            def arrive(step, _):
                x_arrival(lax.rem(me + step, hosts)).wait_recv()
                return 0

            lax.fori_loop(1, hosts, arrive, 0)

            def fill(k, _):
                x_work[k] = x_v[perm[k]]
                return 0

            def fill_moved(k, _):
                source = host_of[k]
                x_work[k] = jnp.where(source == me, x_v[perm[k]], x_recv[source])
                return 0

            lax.fori_loop(CHUNK, CHUNK + BLOCK, fill_moved, 0)
            lax.fori_loop(CHUNK + BLOCK, streams, fill, 0)

        @pl.when(section == 1)
        def _():
            hand_over(chunk).wait_recv()

        project(chunk)

        @pl.when(chunk == 0)
        def _():
            wait_for(out_loads)

        finish(chunk)

        @pl.when(section == 0)
        def _():
            hand_over(chunk).start()

        @pl.when(chunk == BLOCK // CHUNK)
        def _():
            lax.fori_loop(1, hosts, give_back, 0)

        return 0

    lax.fori_loop(0, chunks, turn, 0)

    def returned(step, _):
        y_arrival(lax.rem(me + step, hosts)).wait_recv()
        return 0

    lax.fori_loop(1, hosts, returned, 0)

    def assemble(i, _):
        source = lax.shift_right_arithmetic(anchor[base + i], shift)
        out_ref[i] = jnp.where(source == me, y_work[rank[i]], y_recv[source])
        return 0

    lax.fori_loop(0, streams, assemble, 0)

    def sent(step, _):
        y_copy(lax.rem(me + step, hosts)).wait_send()
        return 0

    lax.fori_loop(1, hosts, sent, 0)

    @pl.when(section == 0)
    def _():
        def x_sent(step, _):
            x_copy(lax.rem(me + step, hosts)).wait_send()
            return 0

        lax.fori_loop(1, hosts, x_sent, 0)
        for chunk in range(chunks):
            hand_over(chunk).wait_send()


def body(new_frames, valid, anchor, context, kept, wqkv, wout, wconv):
    streams, frames, width = new_frames.shape
    hosts = lax.axis_size("stream")
    ctx_rows, kept_rows, taps = context.shape[2], kept.shape[2], wconv.shape[1]
    context = jnp.transpose(context, (0, 2, 1, 3))
    kept = jnp.transpose(kept, (0, 2, 1, 3))
    wconv = jnp.transpose(wconv, (1, 0, 2))
    assert streams == 2 * BLOCK and BLOCK == 2 * CHUNK and lax.axis_size("section") == 2
    assert frames == 16 and taps == kept_rows + 1 and kept_rows % 10 == 0
    assert streams & (streams - 1) == 0
    chunks, blocks, tiles = streams // CHUNK, streams // BLOCK, width // 128
    rows = CHUNK * frames
    bf16, f32, i32 = jnp.bfloat16, jnp.float32, jnp.int32
    vmem, smem = pltpu.VMEM, pltpu.SMEM
    dma = pltpu.SemaphoreType.DMA
    call = pl.pallas_call(
        functools.partial(kernel, hosts, streams, frames, width, ctx_rows, kept_rows, taps),
        out_shape=vmem((streams, frames, width), bf16),
        in_specs=[pl.BlockSpec(memory_space=pltpu.SMEM)] * 2
        + [pl.BlockSpec(memory_space=pl.ANY)] * 6,
        out_specs=pl.BlockSpec(memory_space=pltpu.VMEM),
        scratch_shapes=[
            vmem((streams, frames, width), bf16),
            vmem((ctx_rows, streams, 2 * width), bf16),
            vmem((kept_rows, streams, width), bf16),
            vmem((width, 3 * width), bf16),
            vmem((width, width), bf16),
            vmem((taps, 1, width), f32),
            vmem((streams * frames, ctx_rows * streams), bf16),
            vmem((10 * streams, 10 * streams), bf16),
            vmem((hosts, frames, width), bf16),
            vmem((hosts, frames, width), bf16),
            vmem((hosts, frames, width), bf16),
            vmem((hosts, frames, width), bf16),
            vmem((streams, frames, width), bf16),
            vmem((streams, frames, width), bf16),
            vmem((rows, width), bf16),
            vmem((rows, width), bf16),
            vmem((chunks, 2 * rows, width), bf16),
            vmem((chunks, 2 * rows, width), bf16),
            vmem((rows, width), bf16),
            vmem((tiles, 2 * rows, 2 * rows), f32),
            vmem((tiles, 2 * rows, 2 * rows), bf16),
            vmem((chunks, 2 * rows, 2 * rows), f32),
            vmem((rows, width), f32),
            vmem((blocks, tiles, kept_rows * BLOCK, 128), f32),
            vmem((blocks, tiles, frames * BLOCK, 128), f32),
            vmem((tiles, frames * BLOCK, 128), f32),
            vmem((tiles, frames * BLOCK, 128), f32),
            smem((hosts,), i32),
            smem((hosts,), i32),
            smem((hosts,), i32),
            smem((streams,), i32),
            smem((streams,), i32),
            smem((streams,), i32),
            smem((streams,), i32),
            dma((LOADS,)),
            dma((hosts,)),
            dma((hosts,)),
            dma((hosts,)),
            dma((hosts,)),
            dma((chunks,)),
            dma((chunks,)),
        ],
        compiler_params=pltpu.CompilerParams(
            collective_id=0, has_side_effects=True, vmem_limit_bytes=56 * 1024 * 1024
        ),
        cost_estimate=pl.CostEstimate(
            flops=2 * streams * frames * width * width * 4,
            bytes_accessed=12 * 1024 * 1024,
            transcendentals=streams * frames * width,
        ),
    )
    held = call(anchor, valid, new_frames, context, kept, wqkv, wout, wconv)
    return held[None]


def solution(mesh):
    return jax.shard_map(
        body,
        mesh=mesh,
        in_specs=(
            P(("groups", "stream"), None, None),
            P("groups"),
            P("groups"),
            P("section", ("groups", "stream"), None, None),
            P("section", ("groups", "stream"), None, None),
            P("section", None, None),
            P("section", None, None),
            P("section", None, None),
        ),
        out_specs=P("section", ("groups", "stream"), None, None),
        check_vma=False,
    )
```

```python
import functools

import jax
import jax.numpy as jnp
from jax import lax
from jax.experimental import pallas as pl
from jax.experimental.pallas import tpu as pltpu
from jax.sharding import PartitionSpec as P

HEADS = 16
CHUNK = 4
BLOCK = 8
LOADS = 25
MESH = pl.DeviceIdType.MESH


def kernel(
    hosts, streams, frames, width, ctx_rows, kept_rows, taps,
    anchor, valid, x_hbm, ctx_hbm, kept_hbm, wqkv_hbm, wout_hbm, wconv_hbm, out_ref,
    x_v, ctx_v, kept_v, wqkv, wout, wconv, pick, pick_kept,
    x_send, x_recv, y_send, y_recv, x_work, y_work,
    normed, q_buf, k_buf, v_buf, att_buf, s_buf, p_buf, bias, res_buf, pad_t, conv_t, new_t, conv_o,
    t_send, t_old, t_count, rank, perm, host_of, count_of,
    load_sem, xs_sem, xr_sem, ys_sem, yr_sem, hs_sem, hr_sem,
):
    me = lax.axis_index("stream")
    section = lax.axis_index("section")
    base = me * streams
    rows = CHUNK * frames
    chunks = streams // CHUNK
    blocks = streams // BLOCK
    half = CHUNK * frames
    block_rows = BLOCK * frames
    lanes = 128

    slots = iter(range(LOADS))

    def load(source, target):
        copy = pltpu.make_async_copy(source, target, load_sem.at[next(slots)])
        copy.start()
        return copy

    def load_blocks(source, target, count):
        size = target.shape[0] // count
        spans = [pl.ds(i * size, size) for i in range(count)]
        return [load(source.at[span], target.at[span]) for span in spans]

    def load_weight(source, target, part):
        at = pl.ds(part * width, width)
        return load_blocks(source.at[:, at], target.at[:, at], 4)

    def wait_for(copies):
        for copy in copies:
            copy.wait()

    x_loads = load_blocks(x_hbm, x_v, 2)
    kept_loads = load_blocks(kept_hbm.at[0], kept_v, 3)
    ctx_loads = load_blocks(ctx_hbm.at[0], ctx_v, 3)
    conv_loads = [load(wconv_hbm, wconv)]
    qkv_loads = []
    for part in range(3):
        qkv_loads += load_weight(wqkv_hbm.at[0], wqkv, part)
    out_loads = load_weight(wout_hbm.at[0], wout, 0)

    barrier = pltpu.get_barrier_semaphore()

    def greet(step, _):
        pl.semaphore_signal(
            barrier, inc=1, device_id={"stream": lax.rem(me + step, hosts)}, device_id_type=MESH
        )
        return 0

    lax.fori_loop(1, hosts, greet, 0)
    pl.semaphore_signal(barrier, inc=1, device_id={"section": 1 - section}, device_id_type=MESH)

    shift = streams.bit_length() - 1
    own = [anchor[base + i] for i in range(streams)]
    own_host = [lax.shift_right_arithmetic(a, shift) for a in own]
    short = hosts <= 8

    def scan_send(h, _):
        found = jnp.int32(0)
        for i in range(streams):
            found = jnp.where(own_host[i] == h, i, found)
        t_send[h] = found
        return 0

    lax.fori_loop(0, hosts, scan_send, 0, unroll=short)
    def scan_old(h, _):
        found = jnp.int32(-1)
        for i in range(streams):
            host = lax.shift_right_arithmetic(anchor[h * streams + i], shift)
            found = jnp.where(host == me, i, found)
        slot = h * streams + jnp.maximum(found, 0)
        t_old[h] = jnp.where((found >= 0) & (h != me), anchor[slot] - base, -1)
        t_count[h] = valid[slot]
        return 0

    lax.fori_loop(0, hosts, scan_old, 0, unroll=short)
    stays = [(h == me).astype(jnp.int32) for h in own_host]
    moved = streams - sum(stays)
    gone, left = jnp.int32(CHUNK), jnp.int32(0)
    ranks = []
    for i in range(streams):
        place_left = jnp.where(left < CHUNK, left, left + moved)
        ranks.append(jnp.minimum(jnp.where(own_host[i] == me, place_left, gone), streams - 1))
        rank[i] = ranks[i]
        left = left + stays[i]
        gone = gone + 1 - stays[i]
    for k in range(streams):
        old = jnp.int32(0)
        for i in range(streams):
            old = jnp.where(ranks[i] == k, i, old)
        perm[k] = old
        count = valid[base + old]
        if CHUNK <= k < CHUNK + BLOCK:

            def scan_host(h, found):
                return jnp.where(t_old[h] == old, h, found)

            source = lax.fori_loop(0, hosts, scan_host, me, unroll=short)
            host_of[k] = source
            count = jnp.where(source == me, count, t_count[source])
        count_of[k] = count

    wait_for(x_loads)
    @pl.when(section == 0)
    def _():
        def pack(step, _):
            to = lax.rem(me + step, hosts)
            x_send[to] = x_v[t_send[to]]
            return 0

        lax.fori_loop(1, hosts, pack, 0)

    pl.semaphore_wait(barrier, hosts)

    def x_copy(to):
        return pltpu.make_async_remote_copy(
            src_ref=x_send.at[to], dst_ref=x_recv.at[me],
            send_sem=xs_sem.at[to], recv_sem=xr_sem.at[me],
            device_id={"stream": to}, device_id_type=MESH,
        )

    def x_arrival(source):
        return pltpu.make_async_remote_copy(
            src_ref=x_send.at[source], dst_ref=x_recv.at[source],
            send_sem=xs_sem.at[source], recv_sem=xr_sem.at[source],
            device_id={"stream": source}, device_id_type=MESH,
        )

    def y_copy(to):
        return pltpu.make_async_remote_copy(
            src_ref=y_send.at[to], dst_ref=y_recv.at[me],
            send_sem=ys_sem.at[to], recv_sem=yr_sem.at[me],
            device_id={"stream": to}, device_id_type=MESH,
        )

    def y_arrival(source):
        return pltpu.make_async_remote_copy(
            src_ref=y_send.at[source], dst_ref=y_recv.at[source],
            send_sem=ys_sem.at[source], recv_sem=yr_sem.at[source],
            device_id={"stream": source}, device_id_type=MESH,
        )

    def hand_over(chunk):
        span = pl.ds(chunk * CHUNK, CHUNK)
        return pltpu.make_async_remote_copy(
            src_ref=y_work.at[span], dst_ref=x_work.at[span],
            send_sem=hs_sem.at[chunk], recv_sem=hr_sem.at[chunk],
            device_id={"section": 1 - section}, device_id_type=MESH,
        )

    @pl.when(section == 0)
    def _():
        def send(step, _):
            to = lax.rem(me + step, hosts)
            x_copy(to).start()
            return 0

        lax.fori_loop(1, hosts, send, 0)

    span = ctx_rows * streams
    row = lax.broadcasted_iota(jnp.int32, (frames, span), 0)
    col = lax.broadcasted_iota(jnp.int32, (frames, span), 1)
    slant = col - row * streams
    for k in range(streams):
        pick[pl.ds(k * frames, frames), :] = jnp.where(slant == perm[k], 1.0, 0.0).astype(
            jnp.bfloat16
        )

    steps = 10
    part_rows = steps * BLOCK
    sub = lax.broadcasted_iota(jnp.int32, (BLOCK, steps * streams), 0)
    col = lax.broadcasted_iota(jnp.int32, (BLOCK, steps * streams), 1)
    picks = []
    for block in range(blocks):
        wanted = jnp.zeros((BLOCK, steps * streams), jnp.int32)
        for i in range(BLOCK):
            wanted = jnp.where(sub == i, perm[block * BLOCK + i], wanted)
        for t in range(steps):
            picks.append(jnp.where(col - t * streams == wanted, 1.0, 0.0))
    pick_kept[...] = jnp.concatenate(picks, axis=0).astype(jnp.bfloat16)

    row = lax.broadcasted_iota(jnp.int32, (2 * half, 2 * half), 0)
    col = lax.broadcasted_iota(jnp.int32, (2 * half, 2 * half), 1)
    col_stream = lax.shift_right_arithmetic(col, frames.bit_length() - 1) & (CHUNK - 1)
    same = lax.shift_right_arithmetic(row, frames.bit_length() - 1) & (CHUNK - 1) == col_stream
    col_frame = col & (frames - 1)
    for g in range(chunks):
        limit = jnp.full((2 * half, 2 * half), ctx_rows, jnp.int32)
        for i in range(CHUNK):
            limit = jnp.where((col >= half) & (col_stream == i), count_of[g * CHUNK + i], limit)
        bias[g] = jnp.where(same & (col_frame < limit), 0.0, -1e30)


    wait_for(ctx_loads + kept_loads + conv_loads)

    wide = 512

    def place(i, _):
        for part, to in enumerate((k_buf, v_buf)):
            at = pl.multiple_of(i * wide, wide)
            cached = ctx_v[:, :, pl.ds(part * width + at, wide)].reshape(span, wide)
            cached = jnp.dot(pick[...], cached, preferred_element_type=jnp.float32)
            cached = cached.astype(jnp.bfloat16)
            for g in range(chunks):
                to[g, pl.ds(0, half), pl.ds(at, wide)] = cached[g * half : (g + 1) * half]
        return 0

    lax.fori_loop(0, width // wide, place, 0)

    def place_kept(i, _):
        at = pl.multiple_of(i * 2 * lanes, 2 * lanes)
        for b in range(kept_rows // steps):
            kept = kept_v[pl.ds(b * steps, steps), :, pl.ds(at, 2 * lanes)]
            kept = kept.reshape(steps * streams, 2 * lanes)
            kept = jnp.dot(pick_kept[...], kept, preferred_element_type=jnp.float32)
            for block in range(blocks):
                for w in range(2):
                    pad_t[block, 2 * i + w, pl.ds(b * part_rows, part_rows), :] = kept[
                        block * part_rows : (block + 1) * part_rows, w * lanes : (w + 1) * lanes
                    ]
        return 0

    lax.fori_loop(0, width // (2 * lanes), place_kept, 0)

    def conv_kept(block):
        def step(w, _):
            at = pl.ds(pl.multiple_of(w * lanes, lanes), lanes)
            window = [pad_t[block, w, t * BLOCK : (t + 1) * BLOCK, :] for t in range(kept_rows)]
            totals = [None] * frames
            for j in range(kept_rows):
                tap = jnp.broadcast_to(wconv[j, :, at], (BLOCK, lanes))
                for t in range(min(frames, kept_rows - j)):
                    term = tap * window[t + j]
                    totals[t] = term if j == 0 else totals[t] + term
            for t in range(frames):
                conv_t[block, w, t * BLOCK : (t + 1) * BLOCK, :] = totals[t]
            return 0

        lax.fori_loop(0, width // lanes, step, 0)

    conv_kept(0)

    def project(chunk):
        x = x_work[pl.ds(chunk * CHUNK, CHUNK)].reshape(half, width).astype(jnp.float32)
        centred = x - jnp.mean(x, axis=-1, keepdims=True)
        variance = jnp.mean(centred * centred, axis=-1, keepdims=True)
        normed[...] = (centred * lax.rsqrt(variance + 1e-05)).astype(jnp.bfloat16)
        for part, to in enumerate((q_buf, k_buf, v_buf)):
            got = jnp.dot(
                normed[...], wqkv[:, part * width : (part + 1) * width],
                preferred_element_type=jnp.float32,
            )
            if part == 0:
                to[...] = (got * (width // HEADS) ** (-0.5)).astype(jnp.bfloat16)
            else:
                to[chunk, half:, :] = got.astype(jnp.bfloat16)

    def finish(chunk):
        lane = lax.broadcasted_iota(jnp.int32, (half, lanes), 1)
        first = lane < lanes // 2
        mask = bias[chunk]
        pairs = [pl.ds(p * lanes, lanes) for p in range(width // lanes)]
        for p, at in enumerate(pairs):
            q = q_buf[:, at]
            none = jnp.zeros_like(q)
            q = jnp.concatenate([jnp.where(first, q, none), jnp.where(first, none, q)], axis=0)
            s_buf[p] = lax.dot_general(
                q, k_buf[chunk, :, at], (((1,), (1,)), ((), ())),
                preferred_element_type=jnp.float32,
            )
        for p, at in enumerate(pairs):
            scores = s_buf[p] + mask
            p_buf[p] = jnp.exp(scores - jnp.max(scores, axis=-1, keepdims=True)).astype(
                jnp.bfloat16
            )
        ones = jnp.ones((2 * half, lanes), jnp.bfloat16)
        for p, at in enumerate(pairs):
            values = jnp.concatenate([v_buf[chunk, :, at], ones], axis=1)
            mixed = jnp.dot(p_buf[p], values, preferred_element_type=jnp.float32)
            top = jnp.where(first, mixed[:half, :lanes], mixed[half:, :lanes])
            total = jnp.where(first, mixed[:half, lanes:], mixed[half:, lanes:])
            att_buf[:, at] = (top / total).astype(jnp.bfloat16)

        got = jnp.dot(att_buf[...], wout[...], preferred_element_type=jnp.float32)
        x = x_work[pl.ds(chunk * CHUNK, CHUNK)].reshape(half, width).astype(jnp.float32)
        res_buf[...] = x + got

        block = lax.shift_right_arithmetic(chunk, 1)
        offset = (chunk & 1) * CHUNK
        for s in range(CHUNK):
            own = res_buf[s * frames : (s + 1) * frames, :]
            own = own.astype(jnp.bfloat16).astype(jnp.float32)
            for w in range(width // lanes):
                new_t[w, pl.ds(offset + s, frames, stride=BLOCK), :] = own[
                    :, w * lanes : (w + 1) * lanes
                ]

        def conv_new(w, _):
            at = pl.ds(pl.multiple_of(w * lanes, lanes), lanes)
            window = [new_t[w, t * BLOCK : (t + 1) * BLOCK, :] for t in range(frames)]
            totals = [conv_t[block, w, t * BLOCK : (t + 1) * BLOCK, :] for t in range(frames)]
            for j in range(taps - frames, taps):
                tap = jnp.broadcast_to(wconv[j, :, at], (BLOCK, lanes))
                first_t = kept_rows - j
                for t in range(first_t, frames):
                    totals[t] = totals[t] + tap * window[t - first_t]
            for t in range(frames):
                part = 0.5 * totals[t]
                conv_o[w, t * BLOCK : (t + 1) * BLOCK, :] = part + part * jnp.tanh(part)
            return 0

        lax.fori_loop(0, width // lanes, conv_new, 0)

        frame = lax.broadcasted_iota(jnp.int32, (frames, width), 0)
        for s in range(CHUNK):
            k = chunk * CHUNK + s
            own = res_buf[s * frames : (s + 1) * frames, :]
            own = own + jnp.concatenate(
                [
                    conv_o[w, pl.ds(offset + s, frames, stride=BLOCK), :]
                    for w in range(width // lanes)
                ],
                axis=1,
            )
            y_work[k] = jnp.where(frame < count_of[k], own, 0.0).astype(jnp.bfloat16)

    def give_back(step, _):
        to = lax.rem(me + step, hosts)
        y_send[to] = y_work[rank[jnp.maximum(t_old[to], 0)]]
        y_copy(to).start()
        return 0

    @pl.when(section == 0)
    def _():
        for k in range(CHUNK):
            x_work[k] = x_v[perm[k]]

    @pl.when(section == 1)
    def _():
        conv_kept(1)

    wait_for(qkv_loads)

    def turn(chunk, _):
        @pl.when((section == 0) & (chunk == 1))
        def _():
            conv_kept(1)

            def arrive(step, _):
                x_arrival(lax.rem(me + step, hosts)).wait_recv()
                return 0

            lax.fori_loop(1, hosts, arrive, 0)

            def fill(k, _):
                x_work[k] = x_v[perm[k]]
                return 0

            def fill_moved(k, _):
                source = host_of[k]
                x_work[k] = jnp.where(source == me, x_v[perm[k]], x_recv[source])
                return 0

            lax.fori_loop(CHUNK, CHUNK + BLOCK, fill_moved, 0)
            lax.fori_loop(CHUNK + BLOCK, streams, fill, 0)

        @pl.when(section == 1)
        def _():
            hand_over(chunk).wait_recv()

        project(chunk)

        @pl.when(chunk == 0)
        def _():
            wait_for(out_loads)

        finish(chunk)

        @pl.when(section == 0)
        def _():
            hand_over(chunk).start()

        @pl.when(chunk == BLOCK // CHUNK)
        def _():
            lax.fori_loop(1, hosts, give_back, 0)

        return 0

    lax.fori_loop(0, chunks, turn, 0)

    def returned(step, _):
        y_arrival(lax.rem(me + step, hosts)).wait_recv()
        return 0

    lax.fori_loop(1, hosts, returned, 0)

    def assemble(i, _):
        source = lax.shift_right_arithmetic(anchor[base + i], shift)
        out_ref[i] = jnp.where(source == me, y_work[rank[i]], y_recv[source])
        return 0

    lax.fori_loop(0, streams, assemble, 0)

    def sent(step, _):
        y_copy(lax.rem(me + step, hosts)).wait_send()
        return 0

    lax.fori_loop(1, hosts, sent, 0)

    @pl.when(section == 0)
    def _():
        def x_sent(step, _):
            x_copy(lax.rem(me + step, hosts)).wait_send()
            return 0

        lax.fori_loop(1, hosts, x_sent, 0)
        for chunk in range(chunks):
            hand_over(chunk).wait_send()


def body(new_frames, valid, anchor, context, kept, wqkv, wout, wconv):
    streams, frames, width = new_frames.shape
    hosts = lax.axis_size("stream")
    ctx_rows, kept_rows, taps = context.shape[2], kept.shape[2], wconv.shape[1]
    context = jnp.transpose(context, (0, 2, 1, 3))
    kept = jnp.transpose(kept, (0, 2, 1, 3))
    wconv = jnp.transpose(wconv, (1, 0, 2))
    assert streams == 2 * BLOCK and BLOCK == 2 * CHUNK and lax.axis_size("section") == 2
    assert frames == 16 and taps == kept_rows + 1 and kept_rows % 10 == 0
    assert streams & (streams - 1) == 0
    chunks, blocks, tiles = streams // CHUNK, streams // BLOCK, width // 128
    rows = CHUNK * frames
    bf16, f32, i32 = jnp.bfloat16, jnp.float32, jnp.int32
    vmem, smem = pltpu.VMEM, pltpu.SMEM
    dma = pltpu.SemaphoreType.DMA
    call = pl.pallas_call(
        functools.partial(kernel, hosts, streams, frames, width, ctx_rows, kept_rows, taps),
        out_shape=vmem((streams, frames, width), bf16),
        in_specs=[pl.BlockSpec(memory_space=pltpu.SMEM)] * 2
        + [pl.BlockSpec(memory_space=pl.ANY)] * 6,
        out_specs=pl.BlockSpec(memory_space=pltpu.VMEM),
        scratch_shapes=[
            vmem((streams, frames, width), bf16),
            vmem((ctx_rows, streams, 2 * width), bf16),
            vmem((kept_rows, streams, width), bf16),
            vmem((width, 3 * width), bf16),
            vmem((width, width), bf16),
            vmem((taps, 1, width), f32),
            vmem((streams * frames, ctx_rows * streams), bf16),
            vmem((10 * streams, 10 * streams), bf16),
            vmem((hosts, frames, width), bf16),
            vmem((hosts, frames, width), bf16),
            vmem((hosts, frames, width), bf16),
            vmem((hosts, frames, width), bf16),
            vmem((streams, frames, width), bf16),
            vmem((streams, frames, width), bf16),
            vmem((rows, width), bf16),
            vmem((rows, width), bf16),
            vmem((chunks, 2 * rows, width), bf16),
            vmem((chunks, 2 * rows, width), bf16),
            vmem((rows, width), bf16),
            vmem((tiles, 2 * rows, 2 * rows), f32),
            vmem((tiles, 2 * rows, 2 * rows), bf16),
            vmem((chunks, 2 * rows, 2 * rows), f32),
            vmem((rows, width), f32),
            vmem((blocks, tiles, kept_rows * BLOCK, 128), f32),
            vmem((blocks, tiles, frames * BLOCK, 128), f32),
            vmem((tiles, frames * BLOCK, 128), f32),
            vmem((tiles, frames * BLOCK, 128), f32),
            smem((hosts,), i32),
            smem((hosts,), i32),
            smem((hosts,), i32),
            smem((streams,), i32),
            smem((streams,), i32),
            smem((streams,), i32),
            smem((streams,), i32),
            dma((LOADS,)),
            dma((hosts,)),
            dma((hosts,)),
            dma((hosts,)),
            dma((hosts,)),
            dma((chunks,)),
            dma((chunks,)),
        ],
        compiler_params=pltpu.CompilerParams(
            collective_id=0, has_side_effects=True, vmem_limit_bytes=56 * 1024 * 1024
        ),
        cost_estimate=pl.CostEstimate(
            flops=2 * streams * frames * width * width * 4,
            bytes_accessed=12 * 1024 * 1024,
            transcendentals=streams * frames * width,
        ),
    )
    held = call(anchor, valid, new_frames, context, kept, wqkv, wout, wconv)
    return held[None]


def solution(mesh):
    return jax.shard_map(
        body,
        mesh=mesh,
        in_specs=(
            P(("groups", "stream"), None, None),
            P("groups"),
            P("groups"),
            P("section", ("groups", "stream"), None, None),
            P("section", ("groups", "stream"), None, None),
            P("section", None, None),
            P("section", None, None),
            P("section", None, None),
        ),
        out_specs=P("section", ("groups", "stream"), None, None),
        check_vma=False,
    )
```

```python
import functools

import jax
import jax.numpy as jnp
from jax import lax
from jax.experimental import pallas as pl
from jax.experimental.pallas import tpu as pltpu
from jax.sharding import PartitionSpec as P

HEADS = 16
CHUNK = 8
MESH = pl.DeviceIdType.MESH


def kernel(
    hosts, streams, frames, width, ctx_rows, kept_rows, taps,
    anchor, valid, x_hbm, ctx_hbm, kept_hbm, wqkv_hbm, wout_hbm, wconv_hbm, out_ref,
    x_v, ctx_v, kept_v, wqkv, wout, wconv, pick, pick_kept,
    x_send, x_recv, y_send, y_recv, x_work, y_work,
    normed, q_buf, k_buf, v_buf, att_buf, s_buf, p_buf, bias, res_buf, pad_t, conv_t,
    t_send, t_old, t_count, rank, perm, host_of, count_of,
    load_sem, xs_sem, xr_sem, ys_sem, yr_sem, hs_sem, hr_sem,
):
    me = lax.axis_index("stream")
    section = lax.axis_index("section")
    base = me * streams
    rows = CHUNK * frames
    chunks = streams // CHUNK
    group = 4
    half = group * frames
    lanes = 128

    loads = [
        pltpu.make_async_copy(x_hbm, x_v, load_sem.at[0]),
        pltpu.make_async_copy(kept_hbm.at[0], kept_v, load_sem.at[1]),
        pltpu.make_async_copy(ctx_hbm.at[0], ctx_v, load_sem.at[2]),
        pltpu.make_async_copy(wconv_hbm, wconv, load_sem.at[3]),
        pltpu.make_async_copy(wqkv_hbm.at[0], wqkv, load_sem.at[4]),
        pltpu.make_async_copy(wout_hbm.at[0], wout, load_sem.at[5]),
    ]
    loads[0].start()

    barrier = pltpu.get_barrier_semaphore()

    def greet(step, _):
        pl.semaphore_signal(
            barrier, inc=1, device_id={"stream": lax.rem(me + step, hosts)}, device_id_type=MESH
        )
        return 0

    lax.fori_loop(1, hosts, greet, 0)
    pl.semaphore_signal(barrier, inc=1, device_id={"section": 1 - section}, device_id_type=MESH)

    shift = streams.bit_length() - 1
    own = [anchor[base + i] for i in range(streams)]
    own_host = [lax.shift_right_arithmetic(a, shift) for a in own]
    short = hosts <= 8

    def scan_send(h, _):
        found = jnp.int32(0)
        for i in range(streams):
            found = jnp.where(own_host[i] == h, i, found)
        t_send[h] = found
        return 0

    lax.fori_loop(0, hosts, scan_send, 0, unroll=short)
    loads[0].wait()
    for load in loads[1:]:
        load.start()
    @pl.when(section == 0)
    def _():
        def pack(step, _):
            to = lax.rem(me + step, hosts)
            x_send[to] = x_v[t_send[to]]
            return 0

        lax.fori_loop(1, hosts, pack, 0)

    def scan_old(h, _):
        found = jnp.int32(-1)
        for i in range(streams):
            host = lax.shift_right_arithmetic(anchor[h * streams + i], shift)
            found = jnp.where(host == me, i, found)
        slot = h * streams + jnp.maximum(found, 0)
        t_old[h] = jnp.where((found >= 0) & (h != me), anchor[slot] - base, -1)
        t_count[h] = valid[slot]
        return 0

    lax.fori_loop(0, hosts, scan_old, 0, unroll=short)
    stays = [(h == me).astype(jnp.int32) for h in own_host]
    moved = streams - sum(stays)
    gone, left = jnp.int32(0), moved
    ranks = []
    for i in range(streams):
        ranks.append(jnp.minimum(jnp.where(own_host[i] == me, left, gone), streams - 1))
        rank[i] = ranks[i]
        left = left + stays[i]
        gone = gone + 1 - stays[i]
    for k in range(streams):
        old = jnp.int32(0)
        for i in range(streams):
            old = jnp.where(ranks[i] == k, i, old)
        perm[k] = old
        count = valid[base + old]
        if k < CHUNK:

            def scan_host(h, found):
                return jnp.where(t_old[h] == old, h, found)

            source = lax.fori_loop(0, hosts, scan_host, me, unroll=short)
            host_of[k] = source
            count = jnp.where(source == me, count, t_count[source])
        count_of[k] = count

    span = ctx_rows * streams
    row = lax.broadcasted_iota(jnp.int32, (frames, span), 0)
    col = lax.broadcasted_iota(jnp.int32, (frames, span), 1)
    slant = col - row * streams
    for k in range(streams):
        pick[pl.ds(k * frames, frames), :] = jnp.where(slant == perm[k], 1.0, 0.0).astype(
            jnp.bfloat16
        )

    steps = 10
    part_rows = steps * CHUNK
    sub = lax.broadcasted_iota(jnp.int32, (CHUNK, steps * streams), 0)
    col = lax.broadcasted_iota(jnp.int32, (CHUNK, steps * streams), 1)
    blocks = []
    for chunk in range(chunks):
        wanted = jnp.zeros((CHUNK, steps * streams), jnp.int32)
        for i in range(CHUNK):
            wanted = jnp.where(sub == i, perm[chunk * CHUNK + i], wanted)
        for t in range(steps):
            blocks.append(jnp.where(col - t * streams == wanted, 1.0, 0.0))
    pick_kept[...] = jnp.concatenate(blocks, axis=0).astype(jnp.bfloat16)

    row = lax.broadcasted_iota(jnp.int32, (2 * half, 2 * half), 0)
    col = lax.broadcasted_iota(jnp.int32, (2 * half, 2 * half), 1)
    col_stream = lax.shift_right_arithmetic(col, frames.bit_length() - 1) & (group - 1)
    same = lax.shift_right_arithmetic(row, frames.bit_length() - 1) & (group - 1) == col_stream
    col_frame = col & (frames - 1)
    for g in range(streams // group):
        limit = jnp.full((2 * half, 2 * half), ctx_rows, jnp.int32)
        for i in range(group):
            limit = jnp.where((col >= half) & (col_stream == i), count_of[g * group + i], limit)
        bias[g] = jnp.where(same & (col_frame < limit), 0.0, -1e30)


    pl.semaphore_wait(barrier, hosts)

    def x_copy(to):
        return pltpu.make_async_remote_copy(
            src_ref=x_send.at[to], dst_ref=x_recv.at[me],
            send_sem=xs_sem.at[to], recv_sem=xr_sem.at[me],
            device_id={"stream": to}, device_id_type=MESH,
        )

    def x_arrival(source):
        return pltpu.make_async_remote_copy(
            src_ref=x_send.at[source], dst_ref=x_recv.at[source],
            send_sem=xs_sem.at[source], recv_sem=xr_sem.at[source],
            device_id={"stream": source}, device_id_type=MESH,
        )

    def y_copy(to):
        return pltpu.make_async_remote_copy(
            src_ref=y_send.at[to], dst_ref=y_recv.at[me],
            send_sem=ys_sem.at[to], recv_sem=yr_sem.at[me],
            device_id={"stream": to}, device_id_type=MESH,
        )

    def y_arrival(source):
        return pltpu.make_async_remote_copy(
            src_ref=y_send.at[source], dst_ref=y_recv.at[source],
            send_sem=ys_sem.at[source], recv_sem=yr_sem.at[source],
            device_id={"stream": source}, device_id_type=MESH,
        )

    def hand_over(chunk):
        span = pl.ds(chunk * CHUNK, CHUNK)
        return pltpu.make_async_remote_copy(
            src_ref=y_work.at[span], dst_ref=x_work.at[span],
            send_sem=hs_sem.at[chunk], recv_sem=hr_sem.at[chunk],
            device_id={"section": 1 - section}, device_id_type=MESH,
        )

    @pl.when(section == 0)
    def _():
        def send(step, _):
            to = lax.rem(me + step, hosts)
            x_copy(to).start()
            return 0

        lax.fori_loop(1, hosts, send, 0)

    loads[2].wait()
    loads[1].wait()
    loads[3].wait()

    wide = 512

    def place(i, _):
        for part, to in enumerate((k_buf, v_buf)):
            at = pl.multiple_of(i * wide, wide)
            cached = ctx_v[:, :, pl.ds(part * width + at, wide)].reshape(span, wide)
            cached = jnp.dot(pick[...], cached, preferred_element_type=jnp.float32)
            cached = cached.astype(jnp.bfloat16)
            for g in range(streams // group):
                to[g, pl.ds(0, half), pl.ds(at, wide)] = cached[g * half : (g + 1) * half]
        return 0

    lax.fori_loop(0, width // wide, place, 0)

    def place_kept(i, _):
        at = pl.multiple_of(i * 2 * lanes, 2 * lanes)
        for b in range(kept_rows // steps):
            kept = kept_v[pl.ds(b * steps, steps), :, pl.ds(at, 2 * lanes)]
            kept = kept.reshape(steps * streams, 2 * lanes)
            kept = jnp.dot(pick_kept[...], kept, preferred_element_type=jnp.float32)
            for chunk in range(chunks):
                for w in range(2):
                    pad_t[chunk, 2 * i + w, pl.ds(b * part_rows, part_rows), :] = kept[
                        chunk * part_rows : (chunk + 1) * part_rows, w * lanes : (w + 1) * lanes
                    ]
        return 0

    lax.fori_loop(0, width // (2 * lanes), place_kept, 0)

    def conv_kept(chunk):
        def step(w, _):
            at = pl.ds(pl.multiple_of(w * lanes, lanes), lanes)
            window = [pad_t[chunk, w, t * CHUNK : (t + 1) * CHUNK, :] for t in range(kept_rows)]
            totals = [None] * frames
            for j in range(kept_rows):
                tap = jnp.broadcast_to(wconv[j, :, at], (CHUNK, lanes))
                for t in range(min(frames, kept_rows - j)):
                    term = tap * window[t + j]
                    totals[t] = term if j == 0 else totals[t] + term
            for t in range(frames):
                conv_t[chunk, w, t * CHUNK : (t + 1) * CHUNK, :] = totals[t]
            return 0

        lax.fori_loop(0, width // lanes, step, 0)

    conv_kept(0)

    def project(chunk):
        x = x_work[pl.ds(chunk * CHUNK, CHUNK)].reshape(rows, width).astype(jnp.float32)
        centred = x - jnp.mean(x, axis=-1, keepdims=True)
        variance = jnp.mean(centred * centred, axis=-1, keepdims=True)
        normed[...] = (centred * lax.rsqrt(variance + 1e-05)).astype(jnp.bfloat16)
        tile = width

        def step_of(part):
            def step(i, _):
                at = pl.multiple_of(i * tile, tile)
                got = jnp.dot(
                    normed[...], wqkv[:, pl.ds(part * width + at, tile)],
                    preferred_element_type=jnp.float32,
                )
                if part == 0:
                    q_buf[chunk, :, pl.ds(at, tile)] = (
                        got * (width // HEADS) ** (-0.5)
                    ).astype(jnp.bfloat16)
                else:
                    got = got.astype(jnp.bfloat16)
                    to = k_buf if part == 1 else v_buf
                    for g in range(CHUNK // group):
                        to[chunk * (CHUNK // group) + g, pl.ds(half, half), pl.ds(at, tile)] = got[
                            g * half : (g + 1) * half
                        ]
                return 0

            return step

        for part in range(3):
            lax.fori_loop(0, width // tile, step_of(part), 0)

    def finish(chunk):
        def attend(g, _):
            lane = lax.broadcasted_iota(jnp.int32, (half, lanes), 1)
            first = lane < lanes // 2
            whole = chunk * (CHUNK // group) + g
            at_rows = pl.ds(pl.multiple_of(g * half, half), half)
            mask = bias[whole]

            pairs = [pl.ds(p * lanes, lanes) for p in range(width // lanes)]
            for p, at in enumerate(pairs):
                q = q_buf[chunk, at_rows, at]
                none = jnp.zeros_like(q)
                q = jnp.concatenate([jnp.where(first, q, none), jnp.where(first, none, q)], axis=0)
                s_buf[p] = lax.dot_general(
                    q, k_buf[whole, :, at], (((1,), (1,)), ((), ())),
                    preferred_element_type=jnp.float32,
                )
            for p, at in enumerate(pairs):
                scores = s_buf[p] + mask
                p_buf[p] = jnp.exp(scores - jnp.max(scores, axis=-1, keepdims=True)).astype(
                    jnp.bfloat16
                )
            ones = jnp.ones((2 * half, lanes), jnp.bfloat16)
            for p, at in enumerate(pairs):
                values = jnp.concatenate([v_buf[whole, :, at], ones], axis=1)
                mixed = jnp.dot(p_buf[p], values, preferred_element_type=jnp.float32)
                top = jnp.where(first, mixed[:half, :lanes], mixed[half:, :lanes])
                total = jnp.where(first, mixed[:half, lanes:], mixed[half:, lanes:])
                att_buf[at_rows, at] = (top / total).astype(jnp.bfloat16)
            return 0

        lax.fori_loop(0, CHUNK // group, attend, 0)
        tile = width

        def mix(i, _):
            at = pl.ds(pl.multiple_of(i * tile, tile), tile)
            got = jnp.dot(att_buf[...], wout[:, at], preferred_element_type=jnp.float32)
            x = x_work[pl.ds(chunk * CHUNK, CHUNK), :, at].reshape(rows, tile)
            res_buf[:, at] = x.astype(jnp.float32) + got
            return 0

        lax.fori_loop(0, width // tile, mix, 0)

        def spread(s, _):
            own = res_buf[pl.ds(pl.multiple_of(s * frames, frames), frames), :]
            own = own.astype(jnp.bfloat16).astype(jnp.float32)
            for w in range(width // lanes):
                pad_t[chunk, w, pl.ds(kept_rows * CHUNK + s, frames, stride=CHUNK), :] = own[
                    :, w * lanes : (w + 1) * lanes
                ]
            return 0

        lax.fori_loop(0, CHUNK, spread, 0, unroll=True)

        def conv_new(step, _):
            at = pl.ds(pl.multiple_of(step * lanes, lanes), lanes)
            window = [
                pad_t[chunk, step, (kept_rows + t) * CHUNK : (kept_rows + t + 1) * CHUNK, :]
                for t in range(frames)
            ]
            totals = [conv_t[chunk, step, t * CHUNK : (t + 1) * CHUNK, :] for t in range(frames)]
            for j in range(taps - frames, taps):
                tap = jnp.broadcast_to(wconv[j, :, at], (CHUNK, lanes))
                first_t = kept_rows - j
                for t in range(first_t, frames):
                    totals[t] = totals[t] + tap * window[t - first_t]
            for t in range(frames):
                part = 0.5 * totals[t]
                conv_t[chunk, step, t * CHUNK : (t + 1) * CHUNK, :] = part + part * jnp.tanh(part)
            return 0

        lax.fori_loop(0, width // lanes, conv_new, 0)

        def close(s, _):
            k = chunk * CHUNK + s
            own = res_buf[pl.ds(pl.multiple_of(s * frames, frames), frames), :]
            own = own + jnp.concatenate(
                [
                    conv_t[chunk, w, pl.ds(s, frames, stride=CHUNK), :]
                    for w in range(width // lanes)
                ],
                axis=1,
            )
            frame = lax.broadcasted_iota(jnp.int32, (frames, width), 0)
            y_work[k] = jnp.where(frame < count_of[k], own, 0.0).astype(jnp.bfloat16)
            return 0

        lax.fori_loop(0, CHUNK, close, 0, unroll=True)

    loads[4].wait()

    @pl.when(section == 0)
    def _():
        def arrive(step, _):
            x_arrival(lax.rem(me + step, hosts)).wait_recv()
            return 0

        lax.fori_loop(1, hosts, arrive, 0)

        def mover(k, _):
            source = host_of[k]
            x_work[k] = jnp.where(source == me, x_v[perm[k]], x_recv[source])
            return 0

        lax.fori_loop(0, CHUNK, mover, 0)

        def stayer(k, _):
            x_work[k] = x_v[perm[k]]
            return 0

        lax.fori_loop(CHUNK, streams, stayer, 0)

    @pl.when(section == 1)
    def _():
        conv_kept(1)
        hand_over(0).wait_recv()

    project(0)
    loads[5].wait()
    finish(0)

    @pl.when(section == 0)
    def _():
        hand_over(0).start()

    def give_back(step, _):
        to = lax.rem(me + step, hosts)
        y_send[to] = y_work[rank[jnp.maximum(t_old[to], 0)]]
        y_copy(to).start()
        return 0

    lax.fori_loop(1, hosts, give_back, 0)

    @pl.when(section == 0)
    def _():
        conv_kept(1)

    @pl.when(section == 1)
    def _():
        hand_over(1).wait_recv()

    project(1)
    finish(1)

    @pl.when(section == 0)
    def _():
        hand_over(1).start()

    def returned(step, _):
        y_arrival(lax.rem(me + step, hosts)).wait_recv()
        return 0

    lax.fori_loop(1, hosts, returned, 0)

    def assemble(i, _):
        source = lax.shift_right_arithmetic(anchor[base + i], shift)
        out_ref[i] = jnp.where(source == me, y_work[rank[i]], y_recv[source])
        return 0

    lax.fori_loop(0, streams, assemble, 0)

    def sent(step, _):
        y_copy(lax.rem(me + step, hosts)).wait_send()
        return 0

    lax.fori_loop(1, hosts, sent, 0)

    @pl.when(section == 0)
    def _():
        def x_sent(step, _):
            x_copy(lax.rem(me + step, hosts)).wait_send()
            return 0

        lax.fori_loop(1, hosts, x_sent, 0)
        hand_over(0).wait_send()
        hand_over(1).wait_send()


def body(new_frames, valid, anchor, context, kept, wqkv, wout, wconv):
    streams, frames, width = new_frames.shape
    hosts = lax.axis_size("stream")
    ctx_rows, kept_rows, taps = context.shape[2], kept.shape[2], wconv.shape[1]
    context = jnp.transpose(context, (0, 2, 1, 3))
    kept = jnp.transpose(kept, (0, 2, 1, 3))
    wconv = jnp.transpose(wconv, (1, 0, 2))
    assert streams == 2 * CHUNK and lax.axis_size("section") == 2
    assert frames == 16 and taps == kept_rows + 1 and kept_rows % 10 == 0
    assert streams & (streams - 1) == 0
    chunks, groups = streams // CHUNK, streams // 4
    rows = CHUNK * frames
    bf16, f32, i32 = jnp.bfloat16, jnp.float32, jnp.int32
    vmem, smem = pltpu.VMEM, pltpu.SMEM
    dma = pltpu.SemaphoreType.DMA
    call = pl.pallas_call(
        functools.partial(kernel, hosts, streams, frames, width, ctx_rows, kept_rows, taps),
        out_shape=vmem((streams, frames, width), bf16),
        in_specs=[pl.BlockSpec(memory_space=pltpu.SMEM)] * 2
        + [pl.BlockSpec(memory_space=pl.ANY)] * 6,
        out_specs=pl.BlockSpec(memory_space=pltpu.VMEM),
        scratch_shapes=[
            vmem((streams, frames, width), bf16),
            vmem((ctx_rows, streams, 2 * width), bf16),
            vmem((kept_rows, streams, width), bf16),
            vmem((width, 3 * width), bf16),
            vmem((width, width), bf16),
            vmem((taps, 1, width), f32),
            vmem((streams * frames, ctx_rows * streams), bf16),
            vmem((10 * streams, 10 * streams), bf16),
            vmem((hosts, frames, width), bf16),
            vmem((hosts, frames, width), bf16),
            vmem((hosts, frames, width), bf16),
            vmem((hosts, frames, width), bf16),
            vmem((streams, frames, width), bf16),
            vmem((streams, frames, width), bf16),
            vmem((rows, width), bf16),
            vmem((chunks, rows, width), bf16),
            vmem((groups, 8 * frames, width), bf16),
            vmem((groups, 8 * frames, width), bf16),
            vmem((rows, width), bf16),
            vmem((width // 128, 8 * frames, 8 * frames), f32),
            vmem((width // 128, 8 * frames, 8 * frames), bf16),
            vmem((groups, 8 * frames, 8 * frames), f32),
            vmem((rows, width), f32),
            vmem((chunks, width // 128, (kept_rows + frames) * CHUNK, 128), f32),
            vmem((chunks, width // 128, rows, 128), f32),
            smem((hosts,), i32),
            smem((hosts,), i32),
            smem((hosts,), i32),
            smem((streams,), i32),
            smem((streams,), i32),
            smem((streams,), i32),
            smem((streams,), i32),
            dma((6,)),
            dma((hosts,)),
            dma((hosts,)),
            dma((hosts,)),
            dma((hosts,)),
            dma((chunks,)),
            dma((chunks,)),
        ],
        compiler_params=pltpu.CompilerParams(
            collective_id=0, has_side_effects=True, vmem_limit_bytes=56 * 1024 * 1024
        ),
        cost_estimate=pl.CostEstimate(
            flops=2 * streams * frames * width * width * 4,
            bytes_accessed=12 * 1024 * 1024,
            transcendentals=streams * frames * width,
        ),
    )
    held = call(anchor, valid, new_frames, context, kept, wqkv, wout, wconv)
    return held[None]


def solution(mesh):
    return jax.shard_map(
        body,
        mesh=mesh,
        in_specs=(
            P(("groups", "stream"), None, None),
            P("groups"),
            P("groups"),
            P("section", ("groups", "stream"), None, None),
            P("section", ("groups", "stream"), None, None),
            P("section", None, None),
            P("section", None, None),
            P("section", None, None),
        ),
        out_specs=P("section", ("groups", "stream"), None, None),
        check_vma=False,
    )
```

```python
import functools

import jax
import jax.numpy as jnp
from jax import lax
from jax.experimental import pallas as pl
from jax.experimental.pallas import tpu as pltpu
from jax.sharding import PartitionSpec as P

HEADS = 16
CHUNK = 8
MESH = pl.DeviceIdType.MESH


def kernel(
    hosts, streams, frames, width, ctx_rows, kept_rows, taps,
    anchor, valid, x_hbm, ctx_hbm, kept_hbm, wqkv_hbm, wout_hbm, wconv_hbm, out_ref,
    x_v, ctx_v, kept_v, wqkv, wout, wconv, pick, pick_kept,
    x_send, x_recv, y_send, y_recv, x_work, y_work,
    normed, q_buf, k_buf, v_buf, att_buf, s_buf, p_buf, bias, res_buf, pad_t, conv_t,
    t_send, t_old, t_count, rank, perm, host_of, count_of,
    load_sem, xs_sem, xr_sem, ys_sem, yr_sem, hs_sem, hr_sem,
):
    me = lax.axis_index("stream")
    section = lax.axis_index("section")
    base = me * streams
    rows = CHUNK * frames
    chunks = streams // CHUNK
    group = 4
    half = group * frames
    lanes = 128

    loads = [
        pltpu.make_async_copy(x_hbm, x_v, load_sem.at[0]),
        pltpu.make_async_copy(kept_hbm.at[0], kept_v, load_sem.at[1]),
        pltpu.make_async_copy(ctx_hbm.at[0], ctx_v, load_sem.at[2]),
        pltpu.make_async_copy(wconv_hbm, wconv, load_sem.at[3]),
        pltpu.make_async_copy(wqkv_hbm.at[0], wqkv, load_sem.at[4]),
        pltpu.make_async_copy(wout_hbm.at[0], wout, load_sem.at[5]),
    ]
    loads[0].start()

    barrier = pltpu.get_barrier_semaphore()

    def greet(step, _):
        pl.semaphore_signal(
            barrier, inc=1, device_id={"stream": lax.rem(me + step, hosts)}, device_id_type=MESH
        )
        return 0

    lax.fori_loop(1, hosts, greet, 0)
    pl.semaphore_signal(barrier, inc=1, device_id={"section": 1 - section}, device_id_type=MESH)

    shift = streams.bit_length() - 1
    own = [anchor[base + i] for i in range(streams)]
    own_host = [lax.shift_right_arithmetic(a, shift) for a in own]
    short = hosts <= 8

    def scan_send(h, _):
        found = jnp.int32(0)
        for i in range(streams):
            found = jnp.where(own_host[i] == h, i, found)
        t_send[h] = found
        return 0

    lax.fori_loop(0, hosts, scan_send, 0, unroll=short)
    loads[0].wait()
    for load in loads[1:]:
        load.start()
    @pl.when(section == 0)
    def _():
        def pack(step, _):
            to = lax.rem(me + step, hosts)
            x_send[to] = x_v[t_send[to]]
            return 0

        lax.fori_loop(1, hosts, pack, 0)

    def scan_old(h, _):
        found = jnp.int32(-1)
        for i in range(streams):
            host = lax.shift_right_arithmetic(anchor[h * streams + i], shift)
            found = jnp.where(host == me, i, found)
        slot = h * streams + jnp.maximum(found, 0)
        t_old[h] = jnp.where((found >= 0) & (h != me), anchor[slot] - base, -1)
        t_count[h] = valid[slot]
        return 0

    lax.fori_loop(0, hosts, scan_old, 0, unroll=short)
    stays = [(h == me).astype(jnp.int32) for h in own_host]
    moved = streams - sum(stays)
    gone, left = jnp.int32(0), moved
    ranks = []
    for i in range(streams):
        ranks.append(jnp.minimum(jnp.where(own_host[i] == me, left, gone), streams - 1))
        rank[i] = ranks[i]
        left = left + stays[i]
        gone = gone + 1 - stays[i]
    for k in range(streams):
        old = jnp.int32(0)
        for i in range(streams):
            old = jnp.where(ranks[i] == k, i, old)
        perm[k] = old
        count = valid[base + old]
        if k < CHUNK:

            def scan_host(h, found):
                return jnp.where(t_old[h] == old, h, found)

            source = lax.fori_loop(0, hosts, scan_host, me, unroll=short)
            host_of[k] = source
            count = jnp.where(source == me, count, t_count[source])
        count_of[k] = count

    span = ctx_rows * streams
    row = lax.broadcasted_iota(jnp.int32, (frames, span), 0)
    col = lax.broadcasted_iota(jnp.int32, (frames, span), 1)
    slant = col - row * streams
    for k in range(streams):
        pick[pl.ds(k * frames, frames), :] = jnp.where(slant == perm[k], 1.0, 0.0).astype(
            jnp.bfloat16
        )

    steps = 10
    part_rows = steps * CHUNK
    sub = lax.broadcasted_iota(jnp.int32, (CHUNK, steps * streams), 0)
    col = lax.broadcasted_iota(jnp.int32, (CHUNK, steps * streams), 1)
    blocks = []
    for chunk in range(chunks):
        wanted = jnp.zeros((CHUNK, steps * streams), jnp.int32)
        for i in range(CHUNK):
            wanted = jnp.where(sub == i, perm[chunk * CHUNK + i], wanted)
        for t in range(steps):
            blocks.append(jnp.where(col - t * streams == wanted, 1.0, 0.0))
    pick_kept[...] = jnp.concatenate(blocks, axis=0).astype(jnp.bfloat16)

    row = lax.broadcasted_iota(jnp.int32, (2 * half, 2 * half), 0)
    col = lax.broadcasted_iota(jnp.int32, (2 * half, 2 * half), 1)
    col_stream = lax.shift_right_arithmetic(col, frames.bit_length() - 1) & (group - 1)
    same = lax.shift_right_arithmetic(row, frames.bit_length() - 1) & (group - 1) == col_stream
    col_frame = col & (frames - 1)
    for g in range(streams // group):
        limit = jnp.full((2 * half, 2 * half), ctx_rows, jnp.int32)
        for i in range(group):
            limit = jnp.where((col >= half) & (col_stream == i), count_of[g * group + i], limit)
        bias[g] = jnp.where(same & (col_frame < limit), 0.0, -1e30)


    pl.semaphore_wait(barrier, hosts)

    def x_copy(to):
        return pltpu.make_async_remote_copy(
            src_ref=x_send.at[to], dst_ref=x_recv.at[me],
            send_sem=xs_sem.at[to], recv_sem=xr_sem.at[me],
            device_id={"stream": to}, device_id_type=MESH,
        )

    def x_arrival(source):
        return pltpu.make_async_remote_copy(
            src_ref=x_send.at[source], dst_ref=x_recv.at[source],
            send_sem=xs_sem.at[source], recv_sem=xr_sem.at[source],
            device_id={"stream": source}, device_id_type=MESH,
        )

    def y_copy(to):
        return pltpu.make_async_remote_copy(
            src_ref=y_send.at[to], dst_ref=y_recv.at[me],
            send_sem=ys_sem.at[to], recv_sem=yr_sem.at[me],
            device_id={"stream": to}, device_id_type=MESH,
        )

    def y_arrival(source):
        return pltpu.make_async_remote_copy(
            src_ref=y_send.at[source], dst_ref=y_recv.at[source],
            send_sem=ys_sem.at[source], recv_sem=yr_sem.at[source],
            device_id={"stream": source}, device_id_type=MESH,
        )

    def hand_over(chunk):
        span = pl.ds(chunk * CHUNK, CHUNK)
        return pltpu.make_async_remote_copy(
            src_ref=y_work.at[span], dst_ref=x_work.at[span],
            send_sem=hs_sem.at[chunk], recv_sem=hr_sem.at[chunk],
            device_id={"section": 1 - section}, device_id_type=MESH,
        )

    @pl.when(section == 0)
    def _():
        def send(step, _):
            to = lax.rem(me + step, hosts)
            x_copy(to).start()
            return 0

        lax.fori_loop(1, hosts, send, 0)

    loads[2].wait()
    loads[1].wait()
    loads[3].wait()

    wide = 512

    def place(i, _):
        for part, to in enumerate((k_buf, v_buf)):
            at = pl.multiple_of(i * wide, wide)
            cached = ctx_v[:, :, pl.ds(part * width + at, wide)].reshape(span, wide)
            cached = jnp.dot(pick[...], cached, preferred_element_type=jnp.float32)
            cached = cached.astype(jnp.bfloat16)
            for g in range(streams // group):
                to[g, pl.ds(0, half), pl.ds(at, wide)] = cached[g * half : (g + 1) * half]
        return 0

    lax.fori_loop(0, width // wide, place, 0)

    def place_kept(i, _):
        at = pl.multiple_of(i * 2 * lanes, 2 * lanes)
        for b in range(kept_rows // steps):
            kept = kept_v[pl.ds(b * steps, steps), :, pl.ds(at, 2 * lanes)]
            kept = kept.reshape(steps * streams, 2 * lanes)
            kept = jnp.dot(pick_kept[...], kept, preferred_element_type=jnp.float32)
            for chunk in range(chunks):
                for w in range(2):
                    pad_t[chunk, 2 * i + w, pl.ds(b * part_rows, part_rows), :] = kept[
                        chunk * part_rows : (chunk + 1) * part_rows, w * lanes : (w + 1) * lanes
                    ]
        return 0

    lax.fori_loop(0, width // (2 * lanes), place_kept, 0)

    def conv_kept(chunk):
        def step(w, _):
            at = pl.ds(pl.multiple_of(w * lanes, lanes), lanes)
            window = [pad_t[chunk, w, t * CHUNK : (t + 1) * CHUNK, :] for t in range(kept_rows)]
            totals = [None] * frames
            for j in range(kept_rows):
                tap = jnp.broadcast_to(wconv[j, :, at], (CHUNK, lanes))
                for t in range(min(frames, kept_rows - j)):
                    term = tap * window[t + j]
                    totals[t] = term if j == 0 else totals[t] + term
            for t in range(frames):
                conv_t[chunk, w, t * CHUNK : (t + 1) * CHUNK, :] = totals[t]
            return 0

        lax.fori_loop(0, width // lanes, step, 0)

    for chunk in range(chunks):
        conv_kept(chunk)

    def project(chunk):
        x = x_work[pl.ds(chunk * CHUNK, CHUNK)].reshape(rows, width).astype(jnp.float32)
        centred = x - jnp.mean(x, axis=-1, keepdims=True)
        variance = jnp.mean(centred * centred, axis=-1, keepdims=True)
        normed[...] = (centred * lax.rsqrt(variance + 1e-05)).astype(jnp.bfloat16)
        tile = width

        def step_of(part):
            def step(i, _):
                at = pl.multiple_of(i * tile, tile)
                got = jnp.dot(
                    normed[...], wqkv[:, pl.ds(part * width + at, tile)],
                    preferred_element_type=jnp.float32,
                )
                if part == 0:
                    q_buf[chunk, :, pl.ds(at, tile)] = (
                        got * (width // HEADS) ** (-0.5)
                    ).astype(jnp.bfloat16)
                else:
                    got = got.astype(jnp.bfloat16)
                    to = k_buf if part == 1 else v_buf
                    for g in range(CHUNK // group):
                        to[chunk * (CHUNK // group) + g, pl.ds(half, half), pl.ds(at, tile)] = got[
                            g * half : (g + 1) * half
                        ]
                return 0

            return step

        for part in range(3):
            lax.fori_loop(0, width // tile, step_of(part), 0)

    def finish(chunk):
        def attend(g, _):
            lane = lax.broadcasted_iota(jnp.int32, (half, lanes), 1)
            first = lane < lanes // 2
            whole = chunk * (CHUNK // group) + g
            at_rows = pl.ds(pl.multiple_of(g * half, half), half)
            mask = bias[whole]

            pairs = [pl.ds(p * lanes, lanes) for p in range(width // lanes)]
            for p, at in enumerate(pairs):
                q = q_buf[chunk, at_rows, at]
                none = jnp.zeros_like(q)
                q = jnp.concatenate([jnp.where(first, q, none), jnp.where(first, none, q)], axis=0)
                s_buf[p] = lax.dot_general(
                    q, k_buf[whole, :, at], (((1,), (1,)), ((), ())),
                    preferred_element_type=jnp.float32,
                )
            for p, at in enumerate(pairs):
                scores = s_buf[p] + mask
                p_buf[p] = jnp.exp(scores - jnp.max(scores, axis=-1, keepdims=True)).astype(
                    jnp.bfloat16
                )
            ones = jnp.ones((2 * half, lanes), jnp.bfloat16)
            for p, at in enumerate(pairs):
                values = jnp.concatenate([v_buf[whole, :, at], ones], axis=1)
                mixed = jnp.dot(p_buf[p], values, preferred_element_type=jnp.float32)
                top = jnp.where(first, mixed[:half, :lanes], mixed[half:, :lanes])
                total = jnp.where(first, mixed[:half, lanes:], mixed[half:, lanes:])
                att_buf[at_rows, at] = (top / total).astype(jnp.bfloat16)
            return 0

        lax.fori_loop(0, CHUNK // group, attend, 0)
        tile = width

        def mix(i, _):
            at = pl.ds(pl.multiple_of(i * tile, tile), tile)
            got = jnp.dot(att_buf[...], wout[:, at], preferred_element_type=jnp.float32)
            x = x_work[pl.ds(chunk * CHUNK, CHUNK), :, at].reshape(rows, tile)
            res_buf[:, at] = x.astype(jnp.float32) + got
            return 0

        lax.fori_loop(0, width // tile, mix, 0)

        def spread(s, _):
            own = res_buf[pl.ds(pl.multiple_of(s * frames, frames), frames), :]
            own = own.astype(jnp.bfloat16).astype(jnp.float32)
            for w in range(width // lanes):
                pad_t[chunk, w, pl.ds(kept_rows * CHUNK + s, frames, stride=CHUNK), :] = own[
                    :, w * lanes : (w + 1) * lanes
                ]
            return 0

        lax.fori_loop(0, CHUNK, spread, 0, unroll=True)

        def conv_new(step, _):
            at = pl.ds(pl.multiple_of(step * lanes, lanes), lanes)
            window = [
                pad_t[chunk, step, (kept_rows + t) * CHUNK : (kept_rows + t + 1) * CHUNK, :]
                for t in range(frames)
            ]
            totals = [conv_t[chunk, step, t * CHUNK : (t + 1) * CHUNK, :] for t in range(frames)]
            for j in range(taps - frames, taps):
                tap = jnp.broadcast_to(wconv[j, :, at], (CHUNK, lanes))
                first_t = kept_rows - j
                for t in range(first_t, frames):
                    totals[t] = totals[t] + tap * window[t - first_t]
            for t in range(frames):
                part = 0.5 * totals[t]
                conv_t[chunk, step, t * CHUNK : (t + 1) * CHUNK, :] = part + part * jnp.tanh(part)
            return 0

        lax.fori_loop(0, width // lanes, conv_new, 0)

        def close(s, _):
            k = chunk * CHUNK + s
            own = res_buf[pl.ds(pl.multiple_of(s * frames, frames), frames), :]
            own = own + jnp.concatenate(
                [
                    conv_t[chunk, w, pl.ds(s, frames, stride=CHUNK), :]
                    for w in range(width // lanes)
                ],
                axis=1,
            )
            frame = lax.broadcasted_iota(jnp.int32, (frames, width), 0)
            y_work[k] = jnp.where(frame < count_of[k], own, 0.0).astype(jnp.bfloat16)
            return 0

        lax.fori_loop(0, CHUNK, close, 0, unroll=True)

    loads[4].wait()

    @pl.when(section == 0)
    def _():
        def arrive(step, _):
            x_arrival(lax.rem(me + step, hosts)).wait_recv()
            return 0

        lax.fori_loop(1, hosts, arrive, 0)

        def mover(k, _):
            source = host_of[k]
            x_work[k] = jnp.where(source == me, x_v[perm[k]], x_recv[source])
            return 0

        lax.fori_loop(0, CHUNK, mover, 0)

        def stayer(k, _):
            x_work[k] = x_v[perm[k]]
            return 0

        lax.fori_loop(CHUNK, streams, stayer, 0)

    @pl.when(section == 1)
    def _():
        hand_over(0).wait_recv()

    project(0)
    loads[5].wait()
    finish(0)

    @pl.when(section == 0)
    def _():
        hand_over(0).start()

    def give_back(step, _):
        to = lax.rem(me + step, hosts)
        y_send[to] = y_work[rank[jnp.maximum(t_old[to], 0)]]
        y_copy(to).start()
        return 0

    lax.fori_loop(1, hosts, give_back, 0)

    @pl.when(section == 1)
    def _():
        hand_over(1).wait_recv()

    project(1)
    finish(1)

    @pl.when(section == 0)
    def _():
        hand_over(1).start()

    def returned(step, _):
        y_arrival(lax.rem(me + step, hosts)).wait_recv()
        return 0

    lax.fori_loop(1, hosts, returned, 0)

    def assemble(i, _):
        source = lax.shift_right_arithmetic(anchor[base + i], shift)
        out_ref[i] = jnp.where(source == me, y_work[rank[i]], y_recv[source])
        return 0

    lax.fori_loop(0, streams, assemble, 0)

    def sent(step, _):
        y_copy(lax.rem(me + step, hosts)).wait_send()
        return 0

    lax.fori_loop(1, hosts, sent, 0)

    @pl.when(section == 0)
    def _():
        def x_sent(step, _):
            x_copy(lax.rem(me + step, hosts)).wait_send()
            return 0

        lax.fori_loop(1, hosts, x_sent, 0)
        hand_over(0).wait_send()
        hand_over(1).wait_send()


def body(new_frames, valid, anchor, context, kept, wqkv, wout, wconv):
    streams, frames, width = new_frames.shape
    hosts = lax.axis_size("stream")
    ctx_rows, kept_rows, taps = context.shape[2], kept.shape[2], wconv.shape[1]
    context = jnp.transpose(context, (0, 2, 1, 3))
    kept = jnp.transpose(kept, (0, 2, 1, 3))
    wconv = jnp.transpose(wconv, (1, 0, 2))
    assert streams == 2 * CHUNK and lax.axis_size("section") == 2
    assert frames == 16 and taps == kept_rows + 1 and kept_rows % 10 == 0
    assert streams & (streams - 1) == 0
    chunks, groups = streams // CHUNK, streams // 4
    rows = CHUNK * frames
    bf16, f32, i32 = jnp.bfloat16, jnp.float32, jnp.int32
    vmem, smem = pltpu.VMEM, pltpu.SMEM
    dma = pltpu.SemaphoreType.DMA
    call = pl.pallas_call(
        functools.partial(kernel, hosts, streams, frames, width, ctx_rows, kept_rows, taps),
        out_shape=vmem((streams, frames, width), bf16),
        in_specs=[pl.BlockSpec(memory_space=pltpu.SMEM)] * 2
        + [pl.BlockSpec(memory_space=pl.ANY)] * 6,
        out_specs=pl.BlockSpec(memory_space=pltpu.VMEM),
        scratch_shapes=[
            vmem((streams, frames, width), bf16),
            vmem((ctx_rows, streams, 2 * width), bf16),
            vmem((kept_rows, streams, width), bf16),
            vmem((width, 3 * width), bf16),
            vmem((width, width), bf16),
            vmem((taps, 1, width), f32),
            vmem((streams * frames, ctx_rows * streams), bf16),
            vmem((10 * streams, 10 * streams), bf16),
            vmem((hosts, frames, width), bf16),
            vmem((hosts, frames, width), bf16),
            vmem((hosts, frames, width), bf16),
            vmem((hosts, frames, width), bf16),
            vmem((streams, frames, width), bf16),
            vmem((streams, frames, width), bf16),
            vmem((rows, width), bf16),
            vmem((chunks, rows, width), bf16),
            vmem((groups, 8 * frames, width), bf16),
            vmem((groups, 8 * frames, width), bf16),
            vmem((rows, width), bf16),
            vmem((width // 128, 8 * frames, 8 * frames), f32),
            vmem((width // 128, 8 * frames, 8 * frames), bf16),
            vmem((groups, 8 * frames, 8 * frames), f32),
            vmem((rows, width), f32),
            vmem((chunks, width // 128, (kept_rows + frames) * CHUNK, 128), f32),
            vmem((chunks, width // 128, rows, 128), f32),
            smem((hosts,), i32),
            smem((hosts,), i32),
            smem((hosts,), i32),
            smem((streams,), i32),
            smem((streams,), i32),
            smem((streams,), i32),
            smem((streams,), i32),
            dma((6,)),
            dma((hosts,)),
            dma((hosts,)),
            dma((hosts,)),
            dma((hosts,)),
            dma((chunks,)),
            dma((chunks,)),
        ],
        compiler_params=pltpu.CompilerParams(
            collective_id=0, has_side_effects=True, vmem_limit_bytes=56 * 1024 * 1024
        ),
        cost_estimate=pl.CostEstimate(
            flops=2 * streams * frames * width * width * 4,
            bytes_accessed=12 * 1024 * 1024,
            transcendentals=streams * frames * width,
        ),
    )
    held = call(anchor, valid, new_frames, context, kept, wqkv, wout, wconv)
    return held[None]


def solution(mesh):
    return jax.shard_map(
        body,
        mesh=mesh,
        in_specs=(
            P(("groups", "stream"), None, None),
            P("groups"),
            P("groups"),
            P("section", ("groups", "stream"), None, None),
            P("section", ("groups", "stream"), None, None),
            P("section", None, None),
            P("section", None, None),
            P("section", None, None),
        ),
        out_specs=P("section", ("groups", "stream"), None, None),
        check_vma=False,
    )
```
